32 devices in a mesh: proj: 8 (over z, y), band: 4 (over x, core).
Axes of the slice: x: 2, y: 2, z: 4, core: 2. Of those that a mesh axis runs over, the one named last changes fastest.
Arguments:
- intensities: bfloat16 [8, 2, 4096, 4096], P('proj', None, 'band'), may hold values from 0.1 to 700, as said below
- dist_index: int32 [8, 2], P('proj'), may hold values from 0 to 7, all different within a row
- fresnel_table: float32 [8], replicated, may hold values from 20 to 400
- proj_order: int32 [8], replicated, may hold values from 0 to 7, each once
Outputs:
- sinogram: float32 [4096, 8, 4096], P(('band', 'proj'))
The draws below stay inside these ranges and needn't reach their ends.
Inputs may be any that keep to these rules, and one draw needn't show every extreme that they name: Positive intensities. `dist_index`: the 2 frames of one projection use 2 different settings.
All inputs are finite; a program needn't handle non-finite values.
Results may differ from the reference program's by a relative error of at most 0.0041.
Values may be sent and summed in bfloat16 or wider, within the bound.
No kernel may reach another device: no remote copies, remote signals or barrier semaphores. Data moves between devices by JAX's collectives and lax.ppermute only.
A program may use at most 256 MiB of HBM per device.

```python
import math
import jax
import jax.numpy as jnp
from jax import lax

NROW = 4096
NCOL = 4096
DIST = 2
TABLE = 8
PROJ = 8


def draw_intensities(key, part):
    key = jax.random.fold_in(key, 11)
    keys = jax.random.split(key, 3)
    full_shape = (PROJ, DIST, NROW, NCOL)
    base_level = 0.5
    log_spread = math.log(10.0)
    noise = 0.25 * jnp.clip(jax.random.normal(keys[2], full_shape, jnp.float32), -3.0, 3.0)
    positions = lax.broadcasted_iota(jnp.float32, (1, 1, NROW, 1), 2) / NROW
    ramp_level = base_level + positions
    row_scale = jnp.exp(log_spread * jax.random.uniform(keys[0], (PROJ, DIST, NROW, 1), jnp.float32))
    col_scale = jnp.exp(log_spread * jax.random.uniform(keys[1], (PROJ, DIST, 1, NCOL), jnp.float32))
    return (ramp_level * row_scale * col_scale * (1.0 + noise)).astype(jnp.bfloat16)


def choose_distinct(stream_key, rows, amount, top, lift):
    sequence = jax.random.permutation(jax.random.fold_in(stream_key, 1), amount)
    favour = sequence
    for power in range(3):
        favour = favour * favour // amount
    favour = favour * lift // amount
    chance = jax.random.randint(jax.random.fold_in(stream_key, 2), (rows, amount), 0, 4096) + favour
    fixed_rows = jax.random.permutation(jax.random.fold_in(stream_key, 3), rows)[jnp.arange(amount) % rows]
    chance = jnp.where(jnp.arange(rows)[:, None] == fixed_rows[None, :], 1 << 14, chance)
    score = chance * amount + jnp.arange(amount)
    return lax.top_k(score.astype(jnp.int32), top)[1].astype(jnp.int32)


def setup_inputs(seed: int = 0) -> dict:
    key_of = jax.random.split(jax.random.key(seed), 5)
    intensities = draw_intensities(jax.random.fold_in(key_of[4], 71), 0)
    dist_index = choose_distinct(key_of[1], PROJ, TABLE, DIST, 0)
    fresnel_table = jnp.clip(jnp.exp(jax.random.uniform(key_of[2], (TABLE,), jnp.float32, math.log(20.0), math.log(400.0))), 20.0, 400.0)
    proj_order = jax.random.permutation(key_of[3], PROJ).astype(jnp.int32)
    return {"intensities": intensities, "dist_index": dist_index, "fresnel_table": fresnel_table, "proj_order": proj_order}


alpha_reg = 0.1


def to_half(values):
    return lax.optimization_barrier(values.astype(jnp.bfloat16)).astype(jnp.float32)


def retrieve(image, indices, fresnel_table):
    data = image.astype(jnp.float32)
    mean = jnp.mean(data, axis=(1, 2))
    contrast = data / mean[:, None, None] - 1.0
    packed = contrast[0::2] + 1j * contrast[1::2]
    rows = jnp.fft.fft(packed, axis=-1)
    rows = to_half(jnp.real(rows)) + 1j * to_half(jnp.imag(rows))
    spectra = jnp.fft.fft(rows, axis=-2)
    spec_re = jnp.real(spectra)
    spec_im = jnp.imag(spectra)
    freq_y = jnp.fft.fftfreq(NROW).astype(jnp.float32)
    freq_x = jnp.fft.fftfreq(NCOL).astype(jnp.float32)
    freq_sq = freq_y[:, None] ** 2 + freq_x[None, :] ** 2
    coefficient = fresnel_table[indices]
    sines = jnp.sin(jnp.pi * coefficient[:, None, None] * freq_sq[None, :, :])
    denominator = 2.0 * jnp.sum(sines * sines, axis=0) + alpha_reg
    sines_even = sines[0::2]
    sines_odd = sines[1::2]
    phase_re = jnp.sum(sines_even * spec_re + sines_odd * spec_im, axis=0) / denominator
    phase_im = jnp.sum(sines_even * spec_im - sines_odd * spec_re, axis=0) / denominator
    columns = jnp.fft.ifft(phase_re + 1j * phase_im, axis=0)
    columns = to_half(jnp.real(columns)) + 1j * to_half(jnp.imag(columns))
    return jnp.real(jnp.fft.ifft(columns, axis=-1)).astype(jnp.float32)


def reference(intensities, dist_index, fresnel_table, proj_order):
    phases = lax.map(lambda operands: retrieve(operands[0], operands[1], fresnel_table), (intensities, dist_index))
    inverse_order = jnp.argsort(proj_order)
    return jnp.transpose(phases[inverse_order], (1, 0, 2))
```

```python
import functools
import math

import jax
import jax.numpy as jnp
import numpy as np
from jax import lax
from jax.experimental import pallas as pl
from jax.experimental.pallas import tpu as pltpu
from jax.sharding import PartitionSpec as P

alpha_reg = 0.1
LENGTH = 4096
MAJOR = 32
MINOR = 128
HALF = MAJOR // 2
F32 = jnp.float32
BF16 = jnp.bfloat16
MIB = 1 << 20


def split_table(table):
    high = table.astype(np.float32).astype(jnp.bfloat16)
    low = (table - high.astype(np.float64)).astype(np.float32).astype(jnp.bfloat16)
    return high, low


def as_real(table):
    return np.block([[table.real, table.imag], [-table.imag, table.real]])


@functools.lru_cache(maxsize=None)
def step_tables():
    k = np.arange(MAJOR)[:, None, None]
    b = np.arange(MINOR)[None, :, None]
    s = np.arange(MINOR)[None, None, :]
    return np.exp(-2j * math.pi * ((b * (k + MAJOR * s)) % LENGTH) / LENGTH)


@functools.lru_cache(maxsize=None)
def row_tables():
    step = step_tables()
    out = np.zeros((34, 2 * MINOR, 2 * MINOR))
    for t in range(1, HALF):
        out[2 * t] = as_real(step[t])
        out[2 * t + 1] = as_real(step[MAJOR - t][:, ::-1])
    half = MINOR // 2
    zero = np.zeros((MINOR, half), np.complex128)
    negative = step[0][:, (-np.arange(half)) % MINOR].copy()
    negative[:, 0] = step[0][:, half]
    out[0] = as_real(np.concatenate([step[0][:, :half], zero], 1))
    out[1] = as_real(np.concatenate([negative, zero], 1))
    out[32] = as_real(np.concatenate([zero, step[HALF][:, :half]], 1))
    out[33] = as_real(np.concatenate([zero, step[HALF][:, ::-1][:, :half]], 1))
    return split_table(out)


@functools.lru_cache(maxsize=None)
def column_tables():
    inverse = np.stack([as_real(table) for table in step_tables()])
    return split_table(inverse.transpose(0, 2, 1)), split_table(inverse)


@functools.lru_cache(maxsize=None)
def final_tables():
    step = step_tables()
    out = np.zeros((HALF, 4 * MINOR, 2 * MINOR))
    eye = np.eye(MINOR)
    conjugate = np.diag(np.concatenate([np.ones(MINOR), -np.ones(MINOR)]))
    for t in range(1, HALF):
        turn = np.exp(2j * math.pi * t / MAJOR)
        out[t, : 2 * MINOR] = as_real((1 + 1j * turn) * np.conj(step[t]).T)
        partner = as_real(np.conj(step[HALF - t]).T)
        out[t, 2 * MINOR :] = partner @ conjugate @ as_real((1 - 1j * turn) * eye)
    half = MINOR // 2
    b = np.arange(MINOR)[None, :]
    s = np.arange(half)[:, None]
    even = 2 * math.pi * (b * s) / MINOR
    odd = 2 * math.pi * (b * (HALF + MAJOR * s)) / LENGTH
    first_re, first_im = 2 * np.cos(even), -2 * np.sin(even)
    first_re[0] = 1.0
    first_im[0] = (-1.0) ** np.arange(MINOR)
    second_re, second_im = 2 * np.cos(odd), -2 * np.sin(odd)
    first = np.concatenate([first_re, 0 * second_re, first_im, 0 * second_im], 0)
    second = np.concatenate([0 * first_re, second_re, 0 * first_im, second_im], 0)
    out[0, : 2 * MINOR] = np.concatenate([first + second, first - second], 1)
    return split_table(out / float(LENGTH * LENGTH))


def add(x, y):
    return (x[0] + y[0], x[1] + y[1])


def sub(x, y):
    return (x[0] - y[0], x[1] - y[1])


def turn(x, index, length):
    index = index % length
    re, im = x
    if index == 0:
        return x
    if 4 * index == length:
        return (im, -re)
    if 2 * index == length:
        return (-re, -im)
    if 4 * index == 3 * length:
        return (-im, re)
    angle = 2.0 * math.pi * index / length
    cosine, sine = math.cos(angle), math.sin(angle)
    if 8 * index == length:
        return ((re + im) * cosine, (im - re) * cosine)
    if 8 * index == 3 * length:
        return ((im - re) * sine, (re + im) * (-sine))
    return (re * cosine + im * sine, im * cosine - re * sine)


def dft4(x):
    a, b = add(x[0], x[2]), sub(x[0], x[2])
    c, d = add(x[1], x[3]), sub(x[1], x[3])
    return [add(a, c), (b[0] + d[1], b[1] - d[0]), sub(a, c), (b[0] - d[1], b[1] + d[0])]


def dft8(x):
    even, odd = dft4(x[0::2]), dft4(x[1::2])
    odd = [turn(value, index, 8) for index, value in enumerate(odd)]
    return [add(e, o) for e, o in zip(even, odd)] + [sub(e, o) for e, o in zip(even, odd)]


def dft16(x):
    middle = [dft4([x[4 * a + b] for a in range(4)]) for b in range(4)]
    out = [None] * 16
    for k in range(4):
        part = dft4([turn(middle[b][k], b * k, 16) for b in range(4)])
        for m in range(4):
            out[k + 4 * m] = part[m]
    return out


def dft32(load, store, mid_ref):
    for b in range(8):
        part = dft4([load(8 * a + b) for a in range(4)])
        for k in range(4):
            re, im = turn(part[k], b * k, 32)
            mid_ref[2 * (8 * k + b)] = re
            mid_ref[2 * (8 * k + b) + 1] = im
    for k in range(4):
        part = dft8([(mid_ref[2 * (8 * k + b)], mid_ref[2 * (8 * k + b) + 1]) for b in range(8)])
        for m in range(8):
            store(k + 4 * m, *part[m])


def dot(x, y):
    return jnp.dot(x, y, preferred_element_type=F32)


def row_kernel(chunks, bands, scale_ref, x_ref, high_ref, low_ref, *rest):
    outs, (mid_ref, xs_ref) = rest[:chunks], rest[chunks:]
    rows_here = x_ref.shape[2]
    scale_even, scale_odd = scale_ref[0, 0], scale_ref[0, 1]

    def group(index, carry):
        rows = pl.ds(pl.multiple_of(index * 16, 16), 16)

        def load(a):
            lanes = slice(MINOR * a, MINOR * (a + 1))
            even = x_ref[0, 0, rows, lanes].astype(F32) * scale_even - 1.0
            odd = x_ref[0, 1, rows, lanes].astype(F32) * scale_odd - 1.0
            return even, odd

        def store(k, re, im):
            for place, value in enumerate((re, im)):
                high = value.astype(BF16)
                low = (value - high.astype(F32)).astype(BF16)
                xs_ref[k, rows, MINOR * place : MINOR * (place + 1)] = high
                xs_ref[k, rows, MINOR * (2 + place) : MINOR * (3 + place)] = low

        dft32(load, store, mid_ref)
        return carry

    lax.fori_loop(0, rows_here // 16, group, 0)

    def apply(k, table):
        values = xs_ref[k]
        high = high_ref[table]
        whole = jnp.concatenate([values, values[:, : 2 * MINOR]], axis=1)
        return dot(whole, jnp.concatenate([high, high, low_ref[table]], axis=0))

    width = 2 * MINOR
    outs[0][0, :, :width] = (apply(0, 0) + apply(HALF, 32)).astype(BF16)
    outs[0][0, :, width:] = (apply(0, 1) + apply(HALF, 33)).astype(BF16)
    for chunk in range(chunks):

        def tile(band, carry, chunk=chunk):
            t = chunk * bands + band
            outs[chunk][band, :, :width] = apply(t, 2 * t).astype(BF16)
            outs[chunk][band, :, width:] = apply(MAJOR - t, 2 * t + 1).astype(BF16)
            return carry

        lax.fori_loop(1 if chunk == 0 else 0, bands, tile, 0)


def whole_spec():
    return pl.BlockSpec(memory_space=pltpu.VMEM)


def fixed_spec(shape):
    return pl.BlockSpec(shape, lambda *_: (0,) * len(shape), pipeline_mode=pl.Buffered(1))


def rows_forward(intensities, scale, bands, chunks):
    rows = intensities.shape[2]
    block = min(256, rows)
    high, low = row_tables()
    width = 4 * MINOR
    return pl.pallas_call(
        functools.partial(row_kernel, chunks, bands),
        grid=(rows // block,),
        in_specs=[
            pl.BlockSpec(memory_space=pltpu.SMEM),
            pl.BlockSpec((1, 2, block, LENGTH), lambda i: (0, 0, i, 0)),
            fixed_spec(high.shape),
            fixed_spec(low.shape),
        ],
        out_specs=[pl.BlockSpec((bands, block, width), lambda i: (0, i, 0))] * chunks,
        out_shape=[jax.ShapeDtypeStruct((bands, rows, width), BF16)] * chunks,
        scratch_shapes=[
            pltpu.VMEM((64, 16, MINOR), F32),
            pltpu.VMEM((MAJOR, block, 4 * MINOR), BF16),
        ],
        compiler_params=pltpu.CompilerParams(vmem_limit_bytes=48 * MIB),
        cost_estimate=pl.CostEstimate(
            flops=rows * 34 * 6 * 256 * 256, bytes_accessed=4 * rows * LENGTH * 2 + 9 * MIB, transcendentals=0
        ),
        name="rows_forward",
    )(scale, intensities, jnp.asarray(high), jnp.asarray(low))


def column_kernel(special, first_ref, x_ref, u_ref, v_ref, fh_ref, fl_ref, ih_ref, il_ref, *rest):
    if special:
        nyquist_ref, out_ref, mid_ref, xs_ref, ys_ref = rest
        lane = lax.broadcasted_iota(jnp.int32, (16, MINOR), 1)
        own = (lane == 0) & (first_ref[0] == 1)
    else:
        out_ref, mid_ref, xs_ref, ys_ref = rest

    def forward(index, carry):
        start = pl.multiple_of(index * 16, 16)
        rows = pl.ds(start, 16)
        below = pl.ds(pl.multiple_of(start + MINOR, 16), 16)
        for frame in range(2):

            def load(a, frame=frame):
                pos_re, pos_im, neg_re, neg_im = [
                    x_ref[a, rows, MINOR * i : MINOR * (i + 1)].astype(F32) for i in range(4)
                ]
                if special:
                    neg_re = jnp.where(own, pos_re, neg_re)
                    neg_im = jnp.where(own, pos_im, neg_im)
                if frame == 0:
                    return pos_re + neg_re, pos_im - neg_im
                return pos_im + neg_im, neg_re - pos_re

            def store(k, re, im, frame=frame):
                lanes = slice(MINOR * frame, MINOR * (frame + 1))
                xs_ref[k, rows, lanes] = re.astype(BF16)
                xs_ref[k, below, lanes] = im.astype(BF16)

            dft32(load, store, mid_ref)
        return carry

    lax.fori_loop(0, MINOR // 16, forward, 0)

    sin_even_v, cos_even_v, sin_odd_v, cos_odd_v = [v_ref[i : i + 1, :] for i in range(4)]

    def middle(k, carry):
        values = xs_ref[k]
        table = jnp.concatenate([fh_ref[k], fl_ref[k]], axis=1)
        spectra = dot(table, jnp.concatenate([values, values], axis=0))
        column = u_ref[k]
        sin_even = column[:, 0:1] * cos_even_v + column[:, 1:2] * sin_even_v
        sin_odd = column[:, 2:3] * cos_odd_v + column[:, 3:4] * sin_odd_v
        scale = 1.0 / (4.0 * (sin_even * sin_even + sin_odd * sin_odd) + 2.0 * alpha_reg)
        sin_even = sin_even * scale
        sin_odd = sin_odd * scale
        phase_re = sin_even * spectra[:MINOR, :MINOR] + sin_odd * spectra[:MINOR, MINOR:]
        phase_im = sin_even * spectra[MINOR:, :MINOR] + sin_odd * spectra[MINOR:, MINOR:]
        phase = jnp.concatenate([phase_re.astype(BF16), phase_im.astype(BF16)], axis=0)
        table = jnp.concatenate([ih_ref[k], il_ref[k]], axis=1)
        ys_ref[k] = dot(table, jnp.concatenate([phase, phase], axis=0))
        return carry

    lax.fori_loop(0, MAJOR, middle, 0)

    def inverse(index, carry):
        start = pl.multiple_of(index * 16, 16)
        rows = pl.ds(start, 16)
        below = pl.ds(pl.multiple_of(start + MINOR, 16), 16)

        def load(k):
            return ys_ref[k, below, :], ys_ref[k, rows, :]

        def store(a, im, re):
            if special:
                im = jnp.where(own, nyquist_ref[rows, a : a + 1], im)
            out_ref[a, rows, :MINOR] = re.astype(BF16)
            out_ref[a, rows, MINOR:] = im.astype(BF16)

        dft32(load, store, mid_ref)
        return carry

    lax.fori_loop(0, MINOR // 16, inverse, 0)


def columns(received, first, along_u, along_v, nyquist):
    (fh, fl), (ih, il) = column_tables()
    special = nyquist is not None
    operands = [first, received, along_u, along_v] + [jnp.asarray(t) for t in (fh, fl, ih, il)]
    if special:
        operands.append(nyquist)
    return pl.pallas_call(
        functools.partial(column_kernel, special),
        in_specs=[pl.BlockSpec(memory_space=pltpu.SMEM)] + [whole_spec()] * (len(operands) - 1),
        out_specs=whole_spec(),
        out_shape=jax.ShapeDtypeStruct((MAJOR, MINOR, 2 * MINOR), BF16),
        scratch_shapes=[
            pltpu.VMEM((64, 16, MINOR), F32),
            pltpu.VMEM((MAJOR, 2 * MINOR, 2 * MINOR), BF16),
            pltpu.VMEM((MAJOR, 2 * MINOR, MINOR), F32),
        ],
        compiler_params=pltpu.CompilerParams(vmem_limit_bytes=48 * MIB),
        cost_estimate=pl.CostEstimate(
            flops=32 * 8 * 256 * 256 * 256, bytes_accessed=24 * MIB, transcendentals=0
        ),
        name="columns",
    )(*operands)


def final_kernel(chunks, bands, place_ref, *rest):
    ins, (high_ref, low_ref, out_ref, xs_ref, zs_ref) = rest[:chunks], rest[chunks:]
    place = place_ref[...]
    count = place.shape[0]
    for chunk in range(chunks):

        def arrange(band, carry, chunk=chunk):
            values = ins[chunk][band].reshape(count, 2 * MINOR)
            xs_ref[chunk * bands + band] = dot(place, values).astype(BF16)
            return carry

        lax.fori_loop(0, bands, arrange, 0)

    def tile(t, carry):
        partner = lax.rem(HALF - t, HALF)
        pair = jnp.concatenate([xs_ref[t], xs_ref[partner]], axis=1)
        pair = jnp.concatenate([pair, pair], axis=1)
        zs_ref[t] = dot(pair, jnp.concatenate([high_ref[t], low_ref[t]], axis=0))
        return carry

    lax.fori_loop(0, HALF, tile, 0)

    def group(index, carry):
        rows = pl.ds(pl.multiple_of(index * 8, 8), 8)
        values = [(zs_ref[t, rows, MINOR:], zs_ref[t, rows, :MINOR]) for t in range(HALF)]
        for n, (odd, even) in enumerate(dft16(values)):
            out_ref[rows, MINOR * 2 * n : MINOR * (2 * n + 1)] = even
            out_ref[rows, MINOR * (2 * n + 1) : MINOR * (2 * n + 2)] = odd
        return carry

    lax.fori_loop(0, count // 8, group, 0)


def rows_inverse(received, proj_order, bands):
    chunks = len(received)
    _, projections, rows, width = received[0].shape
    block = min(256 // projections, rows)
    count = block * projections
    high, low = final_tables()
    to = jnp.arange(count, dtype=jnp.int32)
    slot = proj_order[to // block]
    place = (to[:, None] == ((to % block) * projections + slot)[None, :]).astype(BF16)
    result = pl.pallas_call(
        functools.partial(final_kernel, chunks, bands),
        grid=(rows // block,),
        in_specs=[fixed_spec((count, count))]
        + [pl.BlockSpec((bands, projections, block, width), lambda i: (0, 0, i, 0))] * chunks
        + [fixed_spec(high.shape), fixed_spec(low.shape)],
        out_specs=pl.BlockSpec((count, LENGTH), lambda i: (i, 0)),
        out_shape=jax.ShapeDtypeStruct((rows * projections, LENGTH), F32),
        scratch_shapes=[
            pltpu.VMEM((HALF, count, 2 * MINOR), BF16),
            pltpu.VMEM((HALF, count, 2 * MINOR), F32),
        ],
        compiler_params=pltpu.CompilerParams(vmem_limit_bytes=48 * MIB),
        cost_estimate=pl.CostEstimate(
            flops=rows * projections * 16 * 10 * 256 * 256,
            bytes_accessed=rows * projections * LENGTH * 6 + 8 * MIB,
            transcendentals=0,
        ),
        name="rows_inverse",
    )(place, *received, jnp.asarray(high), jnp.asarray(low))
    return result.reshape(rows, projections, LENGTH)


def folded_square(position, length):
    folded = jnp.minimum(position, length - position).astype(F32) / length
    return folded * folded


def nyquist_column(re, im, coefficient):
    side = 64
    index = np.arange(side)
    angle = 2 * math.pi * np.outer(index, index) / side
    cosine, sine = np.cos(angle), np.sin(angle)
    forward = np.stack([np.stack([cosine, -sine], 1), np.stack([sine, cosine], 1)]).astype(np.float32)
    inverse = np.stack([np.stack([cosine, sine], 1), np.stack([-sine, cosine], 1)]).astype(np.float32)
    twist = 2 * math.pi * np.outer(index, index) / LENGTH
    twist_cos, twist_sin = np.cos(twist).astype(np.float32), np.sin(twist).astype(np.float32)
    contract = functools.partial(jnp.einsum, precision=lax.Precision.HIGHEST, preferred_element_type=F32)
    values = jnp.stack([re, im]).reshape(2, side, side)
    values = contract("cab,cadk->dkb", values, forward)
    values = jnp.stack(
        [values[0] * twist_cos + values[1] * twist_sin, values[1] * twist_cos - values[0] * twist_sin]
    )
    values = contract("ckb,cbdm->dkm", values, forward)
    position = (
        lax.broadcasted_iota(jnp.int32, (side, side), 0) + side * lax.broadcasted_iota(jnp.int32, (side, side), 1)
    )
    freq_sq = folded_square(position, LENGTH) + 0.25
    sines = jnp.sin(math.pi * coefficient[:, None, None] * freq_sq)
    scale = 1.0 / (2.0 * (sines[0] * sines[0] + sines[1] * sines[1]) + alpha_reg)
    values = jnp.stack(
        [
            (sines[0] * values[0] + sines[1] * values[1]) * scale,
            (sines[0] * values[1] - sines[1] * values[0]) * scale,
        ]
    )
    values = contract("ckm,cmdb->dkb", values, inverse)
    values = jnp.stack(
        [values[0] * twist_cos - values[1] * twist_sin, values[1] * twist_cos + values[0] * twist_sin]
    )
    column = contract("ckb,cka->ab", values, inverse[:, :, 0, :])
    return column.reshape(MAJOR, MINOR).T


def on_device(intensities, dist_index, fresnel_table, proj_order):
    rows = intensities.shape[2]
    bands = lax.axis_size("band")
    projections = lax.axis_size("proj")
    band = lax.axis_index("band")
    chunks = HALF // bands
    totals = lax.psum(jnp.sum(intensities.astype(F32), axis=(2, 3)), "band")
    scale = (rows * bands * LENGTH) / totals

    spectra = rows_forward(intensities, scale, bands, chunks)

    table_size = fresnel_table.shape[0]
    onehot = (dist_index[0][:, None] == jnp.arange(table_size, dtype=jnp.int32)[None, :]).astype(F32)
    coefficient = jnp.sum(onehot * fresnel_table[None, :], axis=1)
    k_index = lax.broadcasted_iota(jnp.int32, (MAJOR, MINOR), 0)
    s_index = lax.broadcasted_iota(jnp.int32, (MAJOR, MINOR), 1)
    angle_u = math.pi * coefficient[:, None, None] * folded_square(k_index + MAJOR * s_index, LENGTH)
    along_u = jnp.stack([jnp.sin(angle_u[0]), jnp.cos(angle_u[0]), jnp.sin(angle_u[1]), jnp.cos(angle_u[1])], axis=-1)
    tile = jnp.arange(chunks, dtype=jnp.int32)[:, None] * bands + band
    lane = jnp.arange(MINOR, dtype=jnp.int32)[None, :]
    first_tile = jnp.where(lane < MINOR // 2, MAJOR * lane, HALF + MAJOR * (lane - MINOR // 2))
    position_v = jnp.where(tile == 0, first_tile, tile + MAJOR * lane)
    angle_v = math.pi * coefficient[:, None, None] * folded_square(position_v, LENGTH)
    along_v = jnp.stack([jnp.sin(angle_v[0]), jnp.cos(angle_v[0]), jnp.sin(angle_v[1]), jnp.cos(angle_v[1])], axis=1)
    first = (band == 0).astype(jnp.int32).reshape(1)

    received = []
    for chunk in range(chunks):
        pencil = lax.all_to_all(spectra[chunk], "band", split_axis=0, concat_axis=0, tiled=True)
        pencil = pencil.reshape(LENGTH, 4 * MINOR)
        nyquist = None
        if chunk == 0:
            nyquist = nyquist_column(
                pencil[:, 2 * MINOR].astype(F32), pencil[:, 3 * MINOR].astype(F32), coefficient
            )
        phase = columns(
            pencil.reshape(MAJOR, MINOR, 4 * MINOR), first, along_u, along_v[chunk], nyquist
        )
        rows_to = LENGTH // (bands * projections)
        phase = phase.reshape(bands * projections, rows_to, 2 * MINOR)
        back = lax.all_to_all(phase, ("band", "proj"), split_axis=0, concat_axis=0, tiled=True)
        received.append(back.reshape(bands, projections, rows_to, 2 * MINOR))

    return rows_inverse(received, proj_order, bands)


def solution(mesh):
    in_specs = (P("proj", None, "band", None), P("proj", None), P(), P())
    out_specs = P(("band", "proj"), None, None)
    return jax.shard_map(
        on_device, mesh=mesh, in_specs=in_specs, out_specs=out_specs, check_vma=False
    )
```

```python
import functools
import math

import jax
import jax.numpy as jnp
import numpy as np
from jax import lax
from jax.experimental import pallas as pl
from jax.experimental.pallas import tpu as pltpu
from jax.sharding import PartitionSpec as P

alpha_reg = 0.1
LENGTH = 4096
MAJOR = 32
MINOR = 128
HALF = MAJOR // 2
F32 = jnp.float32
BF16 = jnp.bfloat16
MIB = 1 << 20


def split_table(table):
    high = table.astype(np.float32).astype(jnp.bfloat16)
    low = (table - high.astype(np.float64)).astype(np.float32).astype(jnp.bfloat16)
    return high, low


def as_real(table):
    return np.block([[table.real, table.imag], [-table.imag, table.real]])


@functools.lru_cache(maxsize=None)
def step_tables():
    k = np.arange(MAJOR)[:, None, None]
    b = np.arange(MINOR)[None, :, None]
    s = np.arange(MINOR)[None, None, :]
    return np.exp(-2j * math.pi * ((b * (k + MAJOR * s)) % LENGTH) / LENGTH)


@functools.lru_cache(maxsize=None)
def row_tables():
    step = step_tables()
    out = np.zeros((34, 2 * MINOR, 2 * MINOR))
    for t in range(1, HALF):
        out[2 * t] = as_real(step[t])
        out[2 * t + 1] = as_real(step[MAJOR - t][:, ::-1])
    half = MINOR // 2
    zero = np.zeros((MINOR, half), np.complex128)
    negative = step[0][:, (-np.arange(half)) % MINOR].copy()
    negative[:, 0] = step[0][:, half]
    out[0] = as_real(np.concatenate([step[0][:, :half], zero], 1))
    out[1] = as_real(np.concatenate([negative, zero], 1))
    out[32] = as_real(np.concatenate([zero, step[HALF][:, :half]], 1))
    out[33] = as_real(np.concatenate([zero, step[HALF][:, ::-1][:, :half]], 1))
    return split_table(out)


@functools.lru_cache(maxsize=None)
def column_tables():
    inverse = np.stack([as_real(table) for table in step_tables()])
    return split_table(inverse.transpose(0, 2, 1)), split_table(inverse)


@functools.lru_cache(maxsize=None)
def final_tables():
    step = step_tables()
    out = np.zeros((HALF, 4 * MINOR, 2 * MINOR))
    eye = np.eye(MINOR)
    conjugate = np.diag(np.concatenate([np.ones(MINOR), -np.ones(MINOR)]))
    for t in range(1, HALF):
        turn = np.exp(2j * math.pi * t / MAJOR)
        out[t, : 2 * MINOR] = as_real((1 + 1j * turn) * np.conj(step[t]).T)
        partner = as_real(np.conj(step[HALF - t]).T)
        out[t, 2 * MINOR :] = partner @ conjugate @ as_real((1 - 1j * turn) * eye)
    half = MINOR // 2
    b = np.arange(MINOR)[None, :]
    s = np.arange(half)[:, None]
    even = 2 * math.pi * (b * s) / MINOR
    odd = 2 * math.pi * (b * (HALF + MAJOR * s)) / LENGTH
    first_re, first_im = 2 * np.cos(even), -2 * np.sin(even)
    first_re[0] = 1.0
    first_im[0] = (-1.0) ** np.arange(MINOR)
    second_re, second_im = 2 * np.cos(odd), -2 * np.sin(odd)
    first = np.concatenate([first_re, 0 * second_re, first_im, 0 * second_im], 0)
    second = np.concatenate([0 * first_re, second_re, 0 * first_im, second_im], 0)
    out[0, : 2 * MINOR] = np.concatenate([first + second, first - second], 1)
    return split_table(out / float(LENGTH * LENGTH))


def add(x, y):
    return (x[0] + y[0], x[1] + y[1])


def sub(x, y):
    return (x[0] - y[0], x[1] - y[1])


def turn(x, index, length):
    index = index % length
    re, im = x
    if index == 0:
        return x
    if 4 * index == length:
        return (im, -re)
    if 2 * index == length:
        return (-re, -im)
    if 4 * index == 3 * length:
        return (-im, re)
    angle = 2.0 * math.pi * index / length
    cosine, sine = math.cos(angle), math.sin(angle)
    if 8 * index == length:
        return ((re + im) * cosine, (im - re) * cosine)
    if 8 * index == 3 * length:
        return ((im - re) * sine, (re + im) * (-sine))
    return (re * cosine + im * sine, im * cosine - re * sine)


def dft4(x):
    a, b = add(x[0], x[2]), sub(x[0], x[2])
    c, d = add(x[1], x[3]), sub(x[1], x[3])
    return [add(a, c), (b[0] + d[1], b[1] - d[0]), sub(a, c), (b[0] - d[1], b[1] + d[0])]


def dft8(x):
    even, odd = dft4(x[0::2]), dft4(x[1::2])
    odd = [turn(value, index, 8) for index, value in enumerate(odd)]
    return [add(e, o) for e, o in zip(even, odd)] + [sub(e, o) for e, o in zip(even, odd)]


def dft16(x):
    middle = [dft4([x[4 * a + b] for a in range(4)]) for b in range(4)]
    out = [None] * 16
    for k in range(4):
        part = dft4([turn(middle[b][k], b * k, 16) for b in range(4)])
        for m in range(4):
            out[k + 4 * m] = part[m]
    return out


def dft32(load, store, mid_ref):
    for b in range(8):
        part = dft4([load(8 * a + b) for a in range(4)])
        for k in range(4):
            re, im = turn(part[k], b * k, 32)
            mid_ref[2 * (8 * k + b)] = re
            mid_ref[2 * (8 * k + b) + 1] = im
    for k in range(4):
        part = dft8([(mid_ref[2 * (8 * k + b)], mid_ref[2 * (8 * k + b) + 1]) for b in range(8)])
        for m in range(8):
            store(k + 4 * m, *part[m])


def dot(x, y):
    return jnp.dot(x, y, preferred_element_type=F32)


def row_kernel(chunks, bands, band_ref, scale_ref, x_ref, high_hbm, low_hbm, *rest):
    outs = rest[: chunks * bands]
    mid_ref, xs_ref, high_ref, low_ref, sems = rest[chunks * bands :]
    rows_here = x_ref.shape[2]
    band = band_ref[0]
    scale_even, scale_odd = scale_ref[0, 0], scale_ref[0, 1]

    def fetches():
        return [
            pltpu.make_async_copy(high_hbm, high_ref, sems.at[0]),
            pltpu.make_async_copy(low_hbm, low_ref, sems.at[1]),
        ]

    @pl.when(pl.program_id(0) == 0)
    def _():
        for fetch in fetches():
            fetch.start()

    def group(index, carry):
        rows = pl.ds(pl.multiple_of(index * 16, 16), 16)

        def load(a):
            lanes = slice(MINOR * a, MINOR * (a + 1))
            even = x_ref[0, 0, rows, lanes].astype(F32) * scale_even - 1.0
            odd = x_ref[0, 1, rows, lanes].astype(F32) * scale_odd - 1.0
            return even, odd

        def store(k, re, im):
            for place, value in enumerate((re, im)):
                high = value.astype(BF16)
                low = (value - high.astype(F32)).astype(BF16)
                xs_ref[k, rows, MINOR * place : MINOR * (place + 1)] = high
                xs_ref[k, rows, MINOR * (2 + place) : MINOR * (3 + place)] = low

        dft32(load, store, mid_ref)
        return carry

    lax.fori_loop(0, rows_here // 16, group, 0)

    @pl.when(pl.program_id(0) == 0)
    def _():
        for fetch in fetches():
            fetch.wait()

    def apply(k, table):
        values = xs_ref[k]
        high = high_ref[table]
        whole = jnp.concatenate([values, values[:, : 2 * MINOR]], axis=1)
        return dot(whole, jnp.concatenate([high, high, low_ref[table]], axis=0))

    width = 2 * MINOR
    for chunk in range(chunks):
        for offset in range(bands):
            t = chunk * bands + (band ^ offset)
            out_ref = outs[chunk * bands + offset]
            out_ref[:, :width] = apply(t, 2 * t).astype(BF16)
            out_ref[:, width:] = apply(lax.rem(MAJOR - t, MAJOR), 2 * t + 1).astype(BF16)
    for offset in range(bands):

        @pl.when(band == offset)
        def _(offset=offset):
            outs[offset][:, :width] = (apply(0, 0) + apply(HALF, 32)).astype(BF16)
            outs[offset][:, width:] = (apply(0, 1) + apply(HALF, 33)).astype(BF16)


def whole_spec():
    return pl.BlockSpec(memory_space=pltpu.VMEM)


def any_spec():
    return pl.BlockSpec(memory_space=pl.ANY)


def fixed_spec(shape):
    return pl.BlockSpec(shape, lambda *_: (0,) * len(shape), pipeline_mode=pl.Buffered(1))


def rows_forward(intensities, scale, band, bands, chunks, part, parts):
    rows = intensities.shape[2] // parts
    block = min(256, rows)
    blocks = rows // block
    high, low = row_tables()
    width = 4 * MINOR
    count = chunks * bands
    outs = pl.pallas_call(
        functools.partial(row_kernel, chunks, bands),
        grid=(blocks,),
        in_specs=[
            pl.BlockSpec(memory_space=pltpu.SMEM),
            pl.BlockSpec(memory_space=pltpu.SMEM),
            pl.BlockSpec((1, 2, block, LENGTH), lambda i: (0, 0, i + part * blocks, 0)),
            any_spec(),
            any_spec(),
        ],
        out_specs=[pl.BlockSpec((block, width), lambda i: (i, 0))] * count,
        out_shape=[jax.ShapeDtypeStruct((rows, width), BF16)] * count,
        scratch_shapes=[
            pltpu.VMEM((64, 16, MINOR), F32),
            pltpu.VMEM((MAJOR, block, 4 * MINOR), BF16),
            pltpu.VMEM(high.shape, BF16),
            pltpu.VMEM(low.shape, BF16),
            pltpu.SemaphoreType.DMA((2,)),
        ],
        compiler_params=pltpu.CompilerParams(vmem_limit_bytes=48 * MIB),
        cost_estimate=pl.CostEstimate(
            flops=rows * 34 * 6 * 256 * 256, bytes_accessed=4 * rows * LENGTH * 2 + 9 * MIB, transcendentals=0
        ),
        name="rows_forward",
    )(band, scale, intensities, jnp.asarray(high), jnp.asarray(low))
    return [outs[bands * chunk : bands * (chunk + 1)] for chunk in range(chunks)]


def column_kernel(special, bands, parts, band_ref, v_ref, *rest):
    blocks = rest[: bands * parts]
    u_hbm, *table_hbms = rest[bands * parts : bands * parts + 5]
    rest = rest[bands * parts + 5 :]
    band = band_ref[0]
    if special:
        nyquist_ref, out_ref, mid_ref, xs_ref, ys_ref, x_ref, u_ref, fh_ref, fl_ref, ih_ref, il_ref, sems = rest
        lane = lax.broadcasted_iota(jnp.int32, (16, MINOR), 1)
        own = (lane == 0) & (band == 0)
    else:
        out_ref, mid_ref, xs_ref, ys_ref, x_ref, u_ref, fh_ref, fl_ref, ih_ref, il_ref, sems = rest

    fetches = []
    height = MAJOR // (bands * parts)
    for offset in range(bands):
        for part in range(parts):
            index = offset * parts + part
            start = (band ^ offset) * (height * parts) + part * height
            fetches.append(
                pltpu.make_async_copy(blocks[index], x_ref.at[pl.ds(start, height)], sems.at[index])
            )
    late = []
    for index, (source, target) in enumerate(
        zip([u_hbm] + table_hbms, (u_ref, fh_ref, fl_ref, ih_ref, il_ref))
    ):
        late.append(pltpu.make_async_copy(source, target, sems.at[bands * parts + index]))
    for fetch in fetches + late:
        fetch.start()
    for fetch in fetches:
        fetch.wait()

    def forward(index, carry):
        start = pl.multiple_of(index * 16, 16)
        rows = pl.ds(start, 16)
        below = pl.ds(pl.multiple_of(start + MINOR, 16), 16)
        for frame in range(2):

            def load(a, frame=frame):
                pos_re, pos_im, neg_re, neg_im = [
                    x_ref[a, rows, MINOR * i : MINOR * (i + 1)].astype(F32) for i in range(4)
                ]
                if special:
                    neg_re = jnp.where(own, pos_re, neg_re)
                    neg_im = jnp.where(own, pos_im, neg_im)
                if frame == 0:
                    return pos_re + neg_re, pos_im - neg_im
                return pos_im + neg_im, neg_re - pos_re

            def store(k, re, im, frame=frame):
                lanes = slice(MINOR * frame, MINOR * (frame + 1))
                xs_ref[k, rows, lanes] = re.astype(BF16)
                xs_ref[k, below, lanes] = im.astype(BF16)

            dft32(load, store, mid_ref)
        return carry

    lax.fori_loop(0, MINOR // 16, forward, 0)
    for fetch in late:
        fetch.wait()

    sin_even_v, cos_even_v, sin_odd_v, cos_odd_v = [v_ref[i : i + 1, :] for i in range(4)]

    def middle(k):
        values = xs_ref[k]
        table = jnp.concatenate([fh_ref[k], fl_ref[k]], axis=1)
        spectra = dot(table, jnp.concatenate([values, values], axis=0))
        column = u_ref[k]
        sin_even = column[:, 0:1] * cos_even_v + column[:, 1:2] * sin_even_v
        sin_odd = column[:, 2:3] * cos_odd_v + column[:, 3:4] * sin_odd_v
        scale = 1.0 / (4.0 * (sin_even * sin_even + sin_odd * sin_odd) + 2.0 * alpha_reg)
        sin_even = sin_even * scale
        sin_odd = sin_odd * scale
        phase_re = sin_even * spectra[:MINOR, :MINOR] + sin_odd * spectra[:MINOR, MINOR:]
        phase_im = sin_even * spectra[MINOR:, :MINOR] + sin_odd * spectra[MINOR:, MINOR:]
        phase = jnp.concatenate([phase_re.astype(BF16), phase_im.astype(BF16)], axis=0)
        table = jnp.concatenate([ih_ref[k], il_ref[k]], axis=1)
        ys_ref[k] = dot(table, jnp.concatenate([phase, phase], axis=0))

    def middles(index, carry):
        for step in range(4):
            middle(4 * index + step)
        return carry

    lax.fori_loop(0, MAJOR // 4, middles, 0)

    def inverse(index, carry):
        start = pl.multiple_of(index * 16, 16)
        rows = pl.ds(start, 16)
        below = pl.ds(pl.multiple_of(start + MINOR, 16), 16)

        def load(k):
            return ys_ref[k, below, :], ys_ref[k, rows, :]

        def store(a, im, re):
            if special:
                im = jnp.where(own, nyquist_ref[rows, a : a + 1], im)
            out_ref[a, rows, :MINOR] = re.astype(BF16)
            out_ref[a, rows, MINOR:] = im.astype(BF16)

        dft32(load, store, mid_ref)
        return carry

    lax.fori_loop(0, MINOR // 16, inverse, 0)


def columns(blocks, band, along_u, along_v, nyquist, bands, parts):
    (fh, fl), (ih, il) = column_tables()
    special = nyquist is not None
    count = bands * parts
    operands = [band, along_v, *blocks, along_u] + [jnp.asarray(t) for t in (fh, fl, ih, il)]
    in_specs = [pl.BlockSpec(memory_space=pltpu.SMEM), whole_spec()] + [any_spec()] * (count + 5)
    if special:
        operands.append(nyquist)
        in_specs.append(whole_spec())
    return pl.pallas_call(
        functools.partial(column_kernel, special, bands, parts),
        in_specs=in_specs,
        out_specs=whole_spec(),
        out_shape=jax.ShapeDtypeStruct((MAJOR, MINOR, 2 * MINOR), BF16),
        scratch_shapes=[
            pltpu.VMEM((64, 16, MINOR), F32),
            pltpu.VMEM((MAJOR, 2 * MINOR, 2 * MINOR), BF16),
            pltpu.VMEM((MAJOR, 2 * MINOR, MINOR), F32),
            pltpu.VMEM((MAJOR, MINOR, 4 * MINOR), BF16),
            pltpu.VMEM(along_u.shape, F32),
        ]
        + [pltpu.VMEM(fh.shape, BF16)] * 4
        + [pltpu.SemaphoreType.DMA((count + 5,))],
        compiler_params=pltpu.CompilerParams(vmem_limit_bytes=48 * MIB),
        cost_estimate=pl.CostEstimate(
            flops=32 * 8 * 256 * 256 * 256, bytes_accessed=24 * MIB, transcendentals=0
        ),
        name="columns",
    )(*operands)


def final_kernel(chunks, bands, place_ref, *rest):
    ins, (high_ref, low_ref, out_ref, xs_ref, zs_ref) = rest[:chunks], rest[chunks:]
    place = place_ref[...]
    count = place.shape[0]
    for chunk in range(chunks):
        for band in range(bands):
            values = ins[chunk][band].reshape(count, 2 * MINOR)
            xs_ref[chunk * bands + band] = dot(place, values).astype(BF16)

    for t in range(HALF):
        partner = (HALF - t) % HALF
        pair = jnp.concatenate([xs_ref[t], xs_ref[partner]], axis=1)
        pair = jnp.concatenate([pair, pair], axis=1)
        zs_ref[t] = dot(pair, jnp.concatenate([high_ref[t], low_ref[t]], axis=0))

    def group(index, carry):
        for half in range(2):
            rows = pl.ds(pl.multiple_of(index * 16 + 8 * half, 8), 8)
            values = [(zs_ref[t, rows, MINOR:], zs_ref[t, rows, :MINOR]) for t in range(HALF)]
            for n, (odd, even) in enumerate(dft16(values)):
                out_ref[rows, MINOR * 2 * n : MINOR * (2 * n + 1)] = even
                out_ref[rows, MINOR * (2 * n + 1) : MINOR * (2 * n + 2)] = odd
        return carry

    lax.fori_loop(0, count // 16, group, 0)


def rows_inverse(received, proj_order, bands):
    chunks = len(received)
    _, projections, rows, width = received[0].shape
    block = min(256 // projections, rows)
    count = block * projections
    high, low = final_tables()
    to = jnp.arange(count, dtype=jnp.int32)
    slot = proj_order[to // block]
    place = (to[:, None] == ((to % block) * projections + slot)[None, :]).astype(BF16)
    result = pl.pallas_call(
        functools.partial(final_kernel, chunks, bands),
        grid=(rows // block,),
        in_specs=[fixed_spec((count, count))]
        + [pl.BlockSpec((bands, projections, block, width), lambda i: (0, 0, i, 0))] * chunks
        + [fixed_spec(high.shape), fixed_spec(low.shape)],
        out_specs=pl.BlockSpec((count, LENGTH), lambda i: (i, 0)),
        out_shape=jax.ShapeDtypeStruct((rows * projections, LENGTH), F32),
        scratch_shapes=[
            pltpu.VMEM((HALF, count, 2 * MINOR), BF16),
            pltpu.VMEM((HALF, count, 2 * MINOR), F32),
        ],
        compiler_params=pltpu.CompilerParams(vmem_limit_bytes=48 * MIB),
        cost_estimate=pl.CostEstimate(
            flops=rows * projections * 16 * 10 * 256 * 256,
            bytes_accessed=rows * projections * LENGTH * 6 + 8 * MIB,
            transcendentals=0,
        ),
        name="rows_inverse",
    )(place, *received, jnp.asarray(high), jnp.asarray(low))
    return result.reshape(rows, projections, LENGTH)


def folded_square(position, length):
    folded = jnp.minimum(position, length - position).astype(F32) / length
    return folded * folded


def nyquist_column(re, im, coefficient):
    side = 64
    index = np.arange(side)
    angle = 2 * math.pi * np.outer(index, index) / side
    cosine, sine = np.cos(angle), np.sin(angle)
    forward = np.stack([np.stack([cosine, -sine], 1), np.stack([sine, cosine], 1)]).astype(np.float32)
    inverse = np.stack([np.stack([cosine, sine], 1), np.stack([-sine, cosine], 1)]).astype(np.float32)
    twist = 2 * math.pi * np.outer(index, index) / LENGTH
    twist_cos, twist_sin = np.cos(twist).astype(np.float32), np.sin(twist).astype(np.float32)
    contract = functools.partial(jnp.einsum, precision=lax.Precision.HIGHEST, preferred_element_type=F32)
    values = jnp.stack([re, im]).reshape(2, side, side)
    values = contract("cab,cadk->dkb", values, forward)
    values = jnp.stack(
        [values[0] * twist_cos + values[1] * twist_sin, values[1] * twist_cos - values[0] * twist_sin]
    )
    values = contract("ckb,cbdm->dkm", values, forward)
    position = (
        lax.broadcasted_iota(jnp.int32, (side, side), 0) + side * lax.broadcasted_iota(jnp.int32, (side, side), 1)
    )
    freq_sq = folded_square(position, LENGTH) + 0.25
    sines = jnp.sin(math.pi * coefficient[:, None, None] * freq_sq)
    scale = 1.0 / (2.0 * (sines[0] * sines[0] + sines[1] * sines[1]) + alpha_reg)
    values = jnp.stack(
        [
            (sines[0] * values[0] + sines[1] * values[1]) * scale,
            (sines[0] * values[1] - sines[1] * values[0]) * scale,
        ]
    )
    values = contract("ckm,cmdb->dkb", values, inverse)
    values = jnp.stack(
        [values[0] * twist_cos - values[1] * twist_sin, values[1] * twist_cos + values[0] * twist_sin]
    )
    column = contract("ckb,cka->ab", values, inverse[:, :, 0, :])
    return column.reshape(MAJOR, MINOR).T


def on_device(intensities, dist_index, fresnel_table, proj_order):
    rows = intensities.shape[2]
    bands = lax.axis_size("band")
    projections = lax.axis_size("proj")
    band = lax.axis_index("band")
    chunks = HALF // bands
    totals = lax.psum(jnp.sum(intensities.astype(F32), axis=(2, 3)), "band")
    scale = (rows * bands * LENGTH) / totals

    here = jnp.asarray(band, jnp.int32).reshape(1)
    parts = 2
    spectra = [rows_forward(intensities, scale, here, bands, chunks, part, parts) for part in range(parts)]

    table_size = fresnel_table.shape[0]
    onehot = (dist_index[0][:, None] == jnp.arange(table_size, dtype=jnp.int32)[None, :]).astype(F32)
    coefficient = jnp.sum(onehot * fresnel_table[None, :], axis=1)
    k_index = lax.broadcasted_iota(jnp.int32, (MAJOR, MINOR), 0)
    s_index = lax.broadcasted_iota(jnp.int32, (MAJOR, MINOR), 1)
    angle_u = math.pi * coefficient[:, None, None] * folded_square(k_index + MAJOR * s_index, LENGTH)
    along_u = jnp.stack([jnp.sin(angle_u[0]), jnp.cos(angle_u[0]), jnp.sin(angle_u[1]), jnp.cos(angle_u[1])], axis=-1)
    tile = jnp.arange(chunks, dtype=jnp.int32)[:, None] * bands + band
    lane = jnp.arange(MINOR, dtype=jnp.int32)[None, :]
    first_tile = jnp.where(lane < MINOR // 2, MAJOR * lane, HALF + MAJOR * (lane - MINOR // 2))
    position_v = jnp.where(tile == 0, first_tile, tile + MAJOR * lane)
    angle_v = math.pi * coefficient[:, None, None] * folded_square(position_v, LENGTH)
    along_v = jnp.stack([jnp.sin(angle_v[0]), jnp.cos(angle_v[0]), jnp.sin(angle_v[1]), jnp.cos(angle_v[1])], axis=1)

    received = []
    for chunk in range(chunks):
        blocks = []
        for offset in range(bands):
            pairs = [(source, source ^ offset) for source in range(bands)]
            for part in range(parts):
                block = spectra[part][chunk][offset]
                if offset:
                    block = lax.ppermute(block, "band", pairs)
                blocks.append(block)
        nyquist = None
        if chunk == 0:
            sent = jnp.stack([block[:, 2 * MINOR :: MINOR] for block in blocks]).astype(F32)
            sent = sent.reshape(bands, rows, 2)[jnp.arange(bands, dtype=jnp.int32) ^ band]
            nyquist = nyquist_column(sent[:, :, 0], sent[:, :, 1], coefficient)
        blocks = [block.reshape(-1, MINOR, 4 * MINOR) for block in blocks]
        phase = columns(blocks, here, along_u, along_v[chunk], nyquist, bands, parts)
        rows_to = LENGTH // (bands * projections)
        phase = phase.reshape(bands * projections, rows_to, 2 * MINOR)
        back = lax.all_to_all(phase, ("band", "proj"), split_axis=0, concat_axis=0, tiled=True)
        received.append(back.reshape(bands, projections, rows_to, 2 * MINOR))

    return rows_inverse(received, proj_order, bands)


def solution(mesh):
    in_specs = (P("proj", None, "band", None), P("proj", None), P(), P())
    out_specs = P(("band", "proj"), None, None)
    return jax.shard_map(
        on_device, mesh=mesh, in_specs=in_specs, out_specs=out_specs, check_vma=False
    )
```

```python
import functools
import math

import jax
import jax.numpy as jnp
import numpy as np
from jax import lax
from jax.experimental import pallas as pl
from jax.experimental.pallas import tpu as pltpu
from jax.sharding import PartitionSpec as P

alpha_reg = 0.1
LENGTH = 4096
MAJOR = 32
MINOR = 128
HALF = MAJOR // 2
F32 = jnp.float32
BF16 = jnp.bfloat16
MIB = 1 << 20


def split_table(table):
    high = table.astype(np.float32).astype(jnp.bfloat16)
    low = (table - high.astype(np.float64)).astype(np.float32).astype(jnp.bfloat16)
    return high, low


def as_real(table):
    return np.block([[table.real, table.imag], [-table.imag, table.real]])


@functools.lru_cache(maxsize=None)
def step_tables():
    k = np.arange(MAJOR)[:, None, None]
    b = np.arange(MINOR)[None, :, None]
    s = np.arange(MINOR)[None, None, :]
    return np.exp(-2j * math.pi * ((b * (k + MAJOR * s)) % LENGTH) / LENGTH)


@functools.lru_cache(maxsize=None)
def row_tables():
    step = step_tables()
    out = np.zeros((34, 2 * MINOR, 2 * MINOR))
    for t in range(1, HALF):
        out[2 * t] = as_real(step[t])
        out[2 * t + 1] = as_real(step[MAJOR - t][:, ::-1])
    half = MINOR // 2
    zero = np.zeros((MINOR, half), np.complex128)
    negative = step[0][:, (-np.arange(half)) % MINOR].copy()
    negative[:, 0] = step[0][:, half]
    out[0] = as_real(np.concatenate([step[0][:, :half], zero], 1))
    out[1] = as_real(np.concatenate([negative, zero], 1))
    out[32] = as_real(np.concatenate([zero, step[HALF][:, :half]], 1))
    out[33] = as_real(np.concatenate([zero, step[HALF][:, ::-1][:, :half]], 1))
    return split_table(out)


@functools.lru_cache(maxsize=None)
def column_tables():
    inverse = np.stack([as_real(table) for table in step_tables()])
    return split_table(inverse.transpose(0, 2, 1)), split_table(inverse)


@functools.lru_cache(maxsize=None)
def final_tables():
    step = step_tables()
    out = np.zeros((HALF, 4 * MINOR, 2 * MINOR))
    eye = np.eye(MINOR)
    conjugate = np.diag(np.concatenate([np.ones(MINOR), -np.ones(MINOR)]))
    for t in range(1, HALF):
        turn = np.exp(2j * math.pi * t / MAJOR)
        out[t, : 2 * MINOR] = as_real((1 + 1j * turn) * np.conj(step[t]).T)
        partner = as_real(np.conj(step[HALF - t]).T)
        out[t, 2 * MINOR :] = partner @ conjugate @ as_real((1 - 1j * turn) * eye)
    half = MINOR // 2
    b = np.arange(MINOR)[None, :]
    s = np.arange(half)[:, None]
    even = 2 * math.pi * (b * s) / MINOR
    odd = 2 * math.pi * (b * (HALF + MAJOR * s)) / LENGTH
    first_re, first_im = 2 * np.cos(even), -2 * np.sin(even)
    first_re[0] = 1.0
    first_im[0] = (-1.0) ** np.arange(MINOR)
    second_re, second_im = 2 * np.cos(odd), -2 * np.sin(odd)
    first = np.concatenate([first_re, 0 * second_re, first_im, 0 * second_im], 0)
    second = np.concatenate([0 * first_re, second_re, 0 * first_im, second_im], 0)
    out[0, : 2 * MINOR] = np.concatenate([first + second, first - second], 1)
    return split_table(out / float(LENGTH * LENGTH))


def add(x, y):
    return (x[0] + y[0], x[1] + y[1])


def sub(x, y):
    return (x[0] - y[0], x[1] - y[1])


def turn(x, index, length):
    index = index % length
    re, im = x
    if index == 0:
        return x
    if 4 * index == length:
        return (im, -re)
    if 2 * index == length:
        return (-re, -im)
    if 4 * index == 3 * length:
        return (-im, re)
    angle = 2.0 * math.pi * index / length
    cosine, sine = math.cos(angle), math.sin(angle)
    if 8 * index == length:
        return ((re + im) * cosine, (im - re) * cosine)
    if 8 * index == 3 * length:
        return ((im - re) * sine, (re + im) * (-sine))
    return (re * cosine + im * sine, im * cosine - re * sine)


def dft4(x):
    a, b = add(x[0], x[2]), sub(x[0], x[2])
    c, d = add(x[1], x[3]), sub(x[1], x[3])
    return [add(a, c), (b[0] + d[1], b[1] - d[0]), sub(a, c), (b[0] - d[1], b[1] + d[0])]


def dft8(x):
    even, odd = dft4(x[0::2]), dft4(x[1::2])
    odd = [turn(value, index, 8) for index, value in enumerate(odd)]
    return [add(e, o) for e, o in zip(even, odd)] + [sub(e, o) for e, o in zip(even, odd)]


def dft16(x):
    middle = [dft4([x[4 * a + b] for a in range(4)]) for b in range(4)]
    out = [None] * 16
    for k in range(4):
        part = dft4([turn(middle[b][k], b * k, 16) for b in range(4)])
        for m in range(4):
            out[k + 4 * m] = part[m]
    return out


def dft32(load, store, mid_ref):
    for b in range(8):
        part = dft4([load(8 * a + b) for a in range(4)])
        for k in range(4):
            re, im = turn(part[k], b * k, 32)
            mid_ref[2 * (8 * k + b)] = re
            mid_ref[2 * (8 * k + b) + 1] = im
    for k in range(4):
        part = dft8([(mid_ref[2 * (8 * k + b)], mid_ref[2 * (8 * k + b) + 1]) for b in range(8)])
        for m in range(8):
            store(k + 4 * m, *part[m])


def dot(x, y):
    return jnp.dot(x, y, preferred_element_type=F32)


def sum_kernel(x_ref, out_ref, total_ref):
    @pl.when(pl.program_id(0) == 0)
    def _():
        total_ref[...] = jnp.zeros_like(total_ref)

    rows = x_ref.shape[2]
    for frame in range(2):
        values = x_ref[0, frame].astype(F32).reshape(rows // 8, 8, LENGTH)
        total_ref[frame] += jnp.sum(values, axis=0)

    @pl.when(pl.program_id(0) == pl.num_programs(0) - 1)
    def _():
        for frame in range(2):
            out_ref[0, frame] = jnp.sum(total_ref[frame])


def frame_sums(intensities):
    rows = intensities.shape[2]
    block = 128
    return pl.pallas_call(
        sum_kernel,
        grid=(rows // block,),
        in_specs=[pl.BlockSpec((1, 2, block, LENGTH), lambda i: (0, 0, i, 0))],
        out_specs=pl.BlockSpec(memory_space=pltpu.SMEM),
        out_shape=jax.ShapeDtypeStruct((1, 2), F32),
        scratch_shapes=[pltpu.VMEM((2, 8, LENGTH), F32)],
        compiler_params=pltpu.CompilerParams(vmem_limit_bytes=58 * MIB),
        name="frame_sums",
    )(intensities)


def row_kernel(chunks, bands, kept, band_ref, scale_ref, x_ref, high_hbm, low_hbm, *rest):
    rest = rest[kept:]
    outs = rest[: chunks * bands]
    mid_ref, xs_ref, high_ref, low_ref, sems = rest[chunks * bands :]
    rows_here = x_ref.shape[2]
    band = band_ref[0]
    scale_even, scale_odd = scale_ref[0, 0], scale_ref[0, 1]

    def fetches():
        return [
            pltpu.make_async_copy(high_hbm, high_ref, sems.at[0]),
            pltpu.make_async_copy(low_hbm, low_ref, sems.at[1]),
        ]

    @pl.when(pl.program_id(0) == 0)
    def _():
        for fetch in fetches():
            fetch.start()

    def group(index, carry):
        rows = pl.ds(pl.multiple_of(index * 16, 16), 16)

        def load(a):
            lanes = slice(MINOR * a, MINOR * (a + 1))
            even = x_ref[0, 0, rows, lanes].astype(F32) * scale_even - 1.0
            odd = x_ref[0, 1, rows, lanes].astype(F32) * scale_odd - 1.0
            return even, odd

        def store(k, re, im):
            for place, value in enumerate((re, im)):
                high = value.astype(BF16)
                low = (value - high.astype(F32)).astype(BF16)
                xs_ref[k, rows, MINOR * place : MINOR * (place + 1)] = high
                xs_ref[k, rows, MINOR * (2 + place) : MINOR * (3 + place)] = low

        dft32(load, store, mid_ref)
        return carry

    lax.fori_loop(0, rows_here // 16, group, 0)

    @pl.when(pl.program_id(0) == 0)
    def _():
        for fetch in fetches():
            fetch.wait()

    def apply(k, table):
        values = xs_ref[k]
        high = high_ref[table]
        whole = jnp.concatenate([values, values[:, : 2 * MINOR]], axis=1)
        return dot(whole, jnp.concatenate([high, high, low_ref[table]], axis=0))

    width = 2 * MINOR
    for chunk in range(chunks):
        for offset in range(bands):
            t = chunk * bands + (band ^ offset)
            out_ref = outs[chunk * bands + offset]
            out_ref[:, :width] = apply(t, 2 * t).astype(BF16)
            out_ref[:, width:] = apply(lax.rem(MAJOR - t, MAJOR), 2 * t + 1).astype(BF16)
    for offset in range(bands):

        @pl.when(band == offset)
        def _(offset=offset):
            outs[offset][:, :width] = (apply(0, 0) + apply(HALF, 32)).astype(BF16)
            outs[offset][:, width:] = (apply(0, 1) + apply(HALF, 33)).astype(BF16)


def whole_spec():
    return pl.BlockSpec(memory_space=pltpu.VMEM)


def any_spec():
    return pl.BlockSpec(memory_space=pl.ANY)


def fixed_spec(shape):
    return pl.BlockSpec(shape, lambda *_: (0,) * len(shape), pipeline_mode=pl.Buffered(1))


def rows_forward(intensities, scale, band, bands, chunks, part, parts, earlier):
    total = intensities.shape[2]
    rows = total // parts
    block = min(256, rows)
    blocks = rows // block
    high, low = row_tables()
    width = 4 * MINOR
    later = (chunks - 1) * bands
    alone = pl.BlockSpec((block, width), lambda i: (i, 0))
    shared = pl.BlockSpec((block, width), lambda i: (i + part * blocks, 0))
    outs = pl.pallas_call(
        functools.partial(row_kernel, chunks, bands, len(earlier)),
        grid=(blocks,),
        in_specs=[
            pl.BlockSpec(memory_space=pltpu.SMEM),
            pl.BlockSpec(memory_space=pltpu.SMEM),
            pl.BlockSpec((1, 2, block, LENGTH), lambda i: (0, 0, i + part * blocks, 0)),
            any_spec(),
            any_spec(),
        ]
        + [any_spec()] * len(earlier),
        out_specs=[alone] * bands + [shared] * later,
        out_shape=[jax.ShapeDtypeStruct((rows, width), BF16)] * bands
        + [jax.ShapeDtypeStruct((total, width), BF16)] * later,
        scratch_shapes=[
            pltpu.VMEM((64, 16, MINOR), F32),
            pltpu.VMEM((MAJOR, block, 4 * MINOR), BF16),
            pltpu.VMEM(high.shape, BF16),
            pltpu.VMEM(low.shape, BF16),
            pltpu.SemaphoreType.DMA((2,)),
        ],
        input_output_aliases={5 + index: bands + index for index in range(len(earlier))},
        compiler_params=pltpu.CompilerParams(vmem_limit_bytes=58 * MIB),
        cost_estimate=pl.CostEstimate(
            flops=64 * rows * 34 * 6 * 256 * 256, bytes_accessed=4 * rows * LENGTH * 2 + 9 * MIB, transcendentals=0
        ),
        name="rows_forward",
    )(band, scale, intensities, jnp.asarray(high), jnp.asarray(low), *earlier)
    return outs


def column_kernel(special, bands, parts, band_ref, v_ref, *rest):
    blocks = rest[: bands * parts]
    u_hbm, *table_hbms = rest[bands * parts : bands * parts + 5]
    rest = rest[bands * parts + 5 :]
    band = band_ref[0]
    if special:
        nyquist_ref, out_ref, mid_ref, xs_ref, ys_ref, x_ref, u_ref, fh_ref, fl_ref, ih_ref, il_ref, sems = rest
        lane = lax.broadcasted_iota(jnp.int32, (16, MINOR), 1)
        own = (lane == 0) & (band == 0)
    else:
        out_ref, mid_ref, xs_ref, ys_ref, x_ref, u_ref, fh_ref, fl_ref, ih_ref, il_ref, sems = rest

    fetches = []
    height = MAJOR // (bands * parts)
    for offset in range(bands):
        for part in range(parts):
            index = offset * parts + part
            start = (band ^ offset) * (height * parts) + part * height
            fetches.append(
                pltpu.make_async_copy(blocks[index], x_ref.at[pl.ds(start, height)], sems.at[index])
            )
    late = []
    for index, (source, target) in enumerate(
        zip([u_hbm] + table_hbms, (u_ref, fh_ref, fl_ref, ih_ref, il_ref))
    ):
        late.append(pltpu.make_async_copy(source, target, sems.at[bands * parts + index]))
    for fetch in fetches + late:
        fetch.start()
    for fetch in fetches:
        fetch.wait()

    def forward(index, carry):
        start = pl.multiple_of(index * 16, 16)
        rows = pl.ds(start, 16)
        below = pl.ds(pl.multiple_of(start + MINOR, 16), 16)
        for frame in range(2):

            def load(a, frame=frame):
                pos_re, pos_im, neg_re, neg_im = [
                    x_ref[a, rows, MINOR * i : MINOR * (i + 1)].astype(F32) for i in range(4)
                ]
                if special:
                    neg_re = jnp.where(own, pos_re, neg_re)
                    neg_im = jnp.where(own, pos_im, neg_im)
                if frame == 0:
                    return pos_re + neg_re, pos_im - neg_im
                return pos_im + neg_im, neg_re - pos_re

            def store(k, re, im, frame=frame):
                lanes = slice(MINOR * frame, MINOR * (frame + 1))
                xs_ref[k, rows, lanes] = re.astype(BF16)
                xs_ref[k, below, lanes] = im.astype(BF16)

            dft32(load, store, mid_ref)
        return carry

    lax.fori_loop(0, MINOR // 16, forward, 0)
    for fetch in late:
        fetch.wait()

    sin_even_v, cos_even_v, sin_odd_v, cos_odd_v = [v_ref[i : i + 1, :] for i in range(4)]

    def middle(k):
        values = xs_ref[k]
        table = jnp.concatenate([fh_ref[k], fl_ref[k]], axis=1)
        spectra = dot(table, jnp.concatenate([values, values], axis=0))
        column = u_ref[k]
        sin_even = column[:, 0:1] * cos_even_v + column[:, 1:2] * sin_even_v
        sin_odd = column[:, 2:3] * cos_odd_v + column[:, 3:4] * sin_odd_v
        scale = 1.0 / (4.0 * (sin_even * sin_even + sin_odd * sin_odd) + 2.0 * alpha_reg)
        sin_even = sin_even * scale
        sin_odd = sin_odd * scale
        phase_re = sin_even * spectra[:MINOR, :MINOR] + sin_odd * spectra[:MINOR, MINOR:]
        phase_im = sin_even * spectra[MINOR:, :MINOR] + sin_odd * spectra[MINOR:, MINOR:]
        phase = jnp.concatenate([phase_re.astype(BF16), phase_im.astype(BF16)], axis=0)
        table = jnp.concatenate([ih_ref[k], il_ref[k]], axis=1)
        ys_ref[k] = dot(table, jnp.concatenate([phase, phase], axis=0))

    def middles(index, carry):
        for step in range(4):
            middle(4 * index + step)
        return carry

    lax.fori_loop(0, MAJOR // 4, middles, 0)

    def inverse(index, carry):
        start = pl.multiple_of(index * 16, 16)
        rows = pl.ds(start, 16)
        below = pl.ds(pl.multiple_of(start + MINOR, 16), 16)

        def load(k):
            return ys_ref[k, below, :], ys_ref[k, rows, :]

        def store(a, im, re):
            if special:
                im = jnp.where(own, nyquist_ref[rows, a : a + 1], im)
            out_ref[a, rows, :MINOR] = re.astype(BF16)
            out_ref[a, rows, MINOR:] = im.astype(BF16)

        dft32(load, store, mid_ref)
        return carry

    lax.fori_loop(0, MINOR // 16, inverse, 0)


def columns(blocks, band, along_u, along_v, nyquist, bands, parts):
    (fh, fl), (ih, il) = column_tables()
    special = nyquist is not None
    count = bands * parts
    operands = [band, along_v, *blocks, along_u] + [jnp.asarray(t) for t in (fh, fl, ih, il)]
    in_specs = [pl.BlockSpec(memory_space=pltpu.SMEM), whole_spec()] + [any_spec()] * (count + 5)
    if special:
        operands.append(nyquist)
        in_specs.append(whole_spec())
    return pl.pallas_call(
        functools.partial(column_kernel, special, bands, parts),
        in_specs=in_specs,
        out_specs=whole_spec(),
        out_shape=jax.ShapeDtypeStruct((MAJOR, MINOR, 2 * MINOR), BF16),
        scratch_shapes=[
            pltpu.VMEM((64, 16, MINOR), F32),
            pltpu.VMEM((MAJOR, 2 * MINOR, 2 * MINOR), BF16),
            pltpu.VMEM((MAJOR, 2 * MINOR, MINOR), F32),
            pltpu.VMEM((MAJOR, MINOR, 4 * MINOR), BF16),
            pltpu.VMEM(along_u.shape, F32),
        ]
        + [pltpu.VMEM(fh.shape, BF16)] * 4
        + [pltpu.SemaphoreType.DMA((count + 5,))],
        compiler_params=pltpu.CompilerParams(vmem_limit_bytes=58 * MIB),
        cost_estimate=pl.CostEstimate(
            flops=64 * 32 * 8 * 256 * 256 * 256, bytes_accessed=24 * MIB, transcendentals=0
        ),
        name="columns",
    )(*operands)


def final_kernel(chunks, bands, place_ref, *rest):
    ins, (high_ref, low_ref, out_ref, xs_ref, zs_ref) = rest[:chunks], rest[chunks:]
    place = place_ref[...]
    count = place.shape[0]
    for chunk in range(chunks):
        for band in range(bands):
            values = ins[chunk][band].reshape(count, 2 * MINOR)
            xs_ref[chunk * bands + band] = dot(place, values).astype(BF16)

    for t in range(HALF):
        partner = (HALF - t) % HALF
        pair = jnp.concatenate([xs_ref[t], xs_ref[partner]], axis=1)
        pair = jnp.concatenate([pair, pair], axis=1)
        zs_ref[t] = dot(pair, jnp.concatenate([high_ref[t], low_ref[t]], axis=0))

    def group(index, carry):
        for half in range(2):
            rows = pl.ds(pl.multiple_of(index * 16 + 8 * half, 8), 8)
            values = [(zs_ref[t, rows, MINOR:], zs_ref[t, rows, :MINOR]) for t in range(HALF)]
            for n, (odd, even) in enumerate(dft16(values)):
                out_ref[rows, MINOR * 2 * n : MINOR * (2 * n + 1)] = even
                out_ref[rows, MINOR * (2 * n + 1) : MINOR * (2 * n + 2)] = odd
        return carry

    lax.fori_loop(0, count // 16, group, 0)


def rows_inverse(received, proj_order, bands):
    chunks = len(received)
    _, projections, rows, width = received[0].shape
    block = min(256 // projections, rows)
    count = block * projections
    high, low = final_tables()
    to = jnp.arange(count, dtype=jnp.int32)
    slot = proj_order[to // block]
    place = (to[:, None] == ((to % block) * projections + slot)[None, :]).astype(BF16)
    result = pl.pallas_call(
        functools.partial(final_kernel, chunks, bands),
        grid=(rows // block,),
        in_specs=[fixed_spec((count, count))]
        + [pl.BlockSpec((bands, projections, block, width), lambda i: (0, 0, i, 0))] * chunks
        + [fixed_spec(high.shape), fixed_spec(low.shape)],
        out_specs=pl.BlockSpec((count, LENGTH), lambda i: (i, 0)),
        out_shape=jax.ShapeDtypeStruct((rows * projections, LENGTH), F32),
        scratch_shapes=[
            pltpu.VMEM((HALF, count, 2 * MINOR), BF16),
            pltpu.VMEM((HALF, count, 2 * MINOR), F32),
        ],
        compiler_params=pltpu.CompilerParams(vmem_limit_bytes=56 * MIB),
        cost_estimate=pl.CostEstimate(
            flops=rows * projections * 16 * 10 * 256 * 256,
            bytes_accessed=rows * projections * LENGTH * 6 + 8 * MIB,
            transcendentals=0,
        ),
        name="rows_inverse",
    )(place, *received, jnp.asarray(high), jnp.asarray(low))
    return result.reshape(rows, projections, LENGTH)


def folded_square(position, length):
    folded = jnp.minimum(position, length - position).astype(F32) / length
    return folded * folded


def nyquist_column(re, im, coefficient):
    side = 64
    index = np.arange(side)
    angle = 2 * math.pi * np.outer(index, index) / side
    cosine, sine = np.cos(angle), np.sin(angle)
    forward = np.stack([np.stack([cosine, -sine], 1), np.stack([sine, cosine], 1)]).astype(np.float32)
    inverse = np.stack([np.stack([cosine, sine], 1), np.stack([-sine, cosine], 1)]).astype(np.float32)
    twist = 2 * math.pi * np.outer(index, index) / LENGTH
    twist_cos, twist_sin = np.cos(twist).astype(np.float32), np.sin(twist).astype(np.float32)
    contract = functools.partial(jnp.einsum, precision=lax.Precision.HIGHEST, preferred_element_type=F32)
    values = jnp.stack([re, im]).reshape(2, side, side)
    values = contract("cab,cadk->dkb", values, forward)
    values = jnp.stack(
        [values[0] * twist_cos + values[1] * twist_sin, values[1] * twist_cos - values[0] * twist_sin]
    )
    values = contract("ckb,cbdm->dkm", values, forward)
    position = (
        lax.broadcasted_iota(jnp.int32, (side, side), 0) + side * lax.broadcasted_iota(jnp.int32, (side, side), 1)
    )
    freq_sq = folded_square(position, LENGTH) + 0.25
    sines = jnp.sin(math.pi * coefficient[:, None, None] * freq_sq)
    scale = 1.0 / (2.0 * (sines[0] * sines[0] + sines[1] * sines[1]) + alpha_reg)
    values = jnp.stack(
        [
            (sines[0] * values[0] + sines[1] * values[1]) * scale,
            (sines[0] * values[1] - sines[1] * values[0]) * scale,
        ]
    )
    values = contract("ckm,cmdb->dkb", values, inverse)
    values = jnp.stack(
        [values[0] * twist_cos - values[1] * twist_sin, values[1] * twist_cos + values[0] * twist_sin]
    )
    column = contract("ckb,cka->ab", values, inverse[:, :, 0, :])
    return column.reshape(MAJOR, MINOR).T


def on_device(intensities, dist_index, fresnel_table, proj_order):
    rows = intensities.shape[2]
    bands = lax.axis_size("band")
    projections = lax.axis_size("proj")
    band = lax.axis_index("band")
    chunks = HALF // bands
    totals = lax.psum(frame_sums(intensities), "band")
    scale = (rows * bands * LENGTH) / totals

    here = jnp.asarray(band, jnp.int32).reshape(1)
    parts = 2
    firsts, others = [], []
    for part in range(parts):
        outs = rows_forward(intensities, scale, here, bands, chunks, part, parts, others)
        firsts.append(outs[:bands])
        others = outs[bands:]

    table_size = fresnel_table.shape[0]
    onehot = (dist_index[0][:, None] == jnp.arange(table_size, dtype=jnp.int32)[None, :]).astype(F32)
    coefficient = jnp.sum(onehot * fresnel_table[None, :], axis=1)
    k_index = lax.broadcasted_iota(jnp.int32, (MAJOR, MINOR), 0)
    s_index = lax.broadcasted_iota(jnp.int32, (MAJOR, MINOR), 1)
    angle_u = math.pi * coefficient[:, None, None] * folded_square(k_index + MAJOR * s_index, LENGTH)
    along_u = jnp.stack([jnp.sin(angle_u[0]), jnp.cos(angle_u[0]), jnp.sin(angle_u[1]), jnp.cos(angle_u[1])], axis=-1)
    tile = jnp.arange(chunks, dtype=jnp.int32)[:, None] * bands + band
    lane = jnp.arange(MINOR, dtype=jnp.int32)[None, :]
    first_tile = jnp.where(lane < MINOR // 2, MAJOR * lane, HALF + MAJOR * (lane - MINOR // 2))
    position_v = jnp.where(tile == 0, first_tile, tile + MAJOR * lane)
    angle_v = math.pi * coefficient[:, None, None] * folded_square(position_v, LENGTH)
    along_v = jnp.stack([jnp.sin(angle_v[0]), jnp.cos(angle_v[0]), jnp.sin(angle_v[1]), jnp.cos(angle_v[1])], axis=1)

    received = []
    for chunk in range(chunks):
        blocks = []
        for offset in range(bands):
            pairs = [(source, source ^ offset) for source in range(bands)]
            if chunk == 0:
                sources = [first[offset] for first in firsts]
            else:
                sources = [others[(chunk - 1) * bands + offset]]
            for block in sources:
                blocks.append(lax.ppermute(block, "band", pairs) if offset else block)
        nyquist = None
        if chunk == 0:
            sent = jnp.stack([block[:, 2 * MINOR :: MINOR] for block in blocks]).astype(F32)
            sent = sent.reshape(bands, rows, 2)[jnp.arange(bands, dtype=jnp.int32) ^ band]
            nyquist = nyquist_column(sent[:, :, 0], sent[:, :, 1], coefficient)
        blocks = [block.reshape(-1, MINOR, 4 * MINOR) for block in blocks]
        phase = columns(blocks, here, along_u, along_v[chunk], nyquist, bands, len(blocks) // bands)
        rows_to = LENGTH // (bands * projections)
        phase = phase.reshape(bands * projections, rows_to, 2 * MINOR)
        back = lax.all_to_all(phase, ("band", "proj"), split_axis=0, concat_axis=0, tiled=True)
        received.append(back.reshape(bands, projections, rows_to, 2 * MINOR))

    return rows_inverse(received, proj_order, bands)


def solution(mesh):
    in_specs = (P("proj", None, "band", None), P("proj", None), P(), P())
    out_specs = P(("band", "proj"), None, None)
    return jax.shard_map(
        on_device, mesh=mesh, in_specs=in_specs, out_specs=out_specs, check_vma=False
    )
```

```python
import functools
import math

import jax
import jax.numpy as jnp
import numpy as np
from jax import lax
from jax.experimental import pallas as pl
from jax.experimental.pallas import tpu as pltpu
from jax.sharding import PartitionSpec as P

alpha_reg = 0.1
LENGTH = 4096
MAJOR = 32
MINOR = 128
HALF = MAJOR // 2
TILES = 2
F32 = jnp.float32
BF16 = jnp.bfloat16
MIB = 1 << 20


def split_table(table):
    high = table.astype(np.float32).astype(jnp.bfloat16)
    low = (table - high.astype(np.float64)).astype(np.float32).astype(jnp.bfloat16)
    return high, low


def as_real(table):
    return np.block([[table.real, table.imag], [-table.imag, table.real]])


@functools.lru_cache(maxsize=None)
def step_tables():
    k = np.arange(MAJOR)[:, None, None]
    b = np.arange(MINOR)[None, :, None]
    s = np.arange(MINOR)[None, None, :]
    return np.exp(-2j * math.pi * ((b * (k + MAJOR * s)) % LENGTH) / LENGTH)


@functools.lru_cache(maxsize=None)
def row_tables():
    step = step_tables()
    out = np.zeros((34, 2 * MINOR, 2 * MINOR))
    for t in range(1, HALF):
        out[2 * t] = as_real(step[t])
        out[2 * t + 1] = as_real(step[MAJOR - t][:, ::-1])
    half = MINOR // 2
    zero = np.zeros((MINOR, half), np.complex128)
    negative = step[0][:, (-np.arange(half)) % MINOR].copy()
    negative[:, 0] = step[0][:, half]
    out[0] = as_real(np.concatenate([step[0][:, :half], zero], 1))
    out[1] = as_real(np.concatenate([negative, zero], 1))
    out[32] = as_real(np.concatenate([zero, step[HALF][:, :half]], 1))
    out[33] = as_real(np.concatenate([zero, step[HALF][:, ::-1][:, :half]], 1))
    return split_table(out)


@functools.lru_cache(maxsize=None)
def column_tables():
    inverse = np.stack([as_real(table) for table in step_tables()])
    return split_table(inverse.transpose(0, 2, 1)), split_table(inverse)


@functools.lru_cache(maxsize=None)
def final_tables():
    step = step_tables()
    out = np.zeros((HALF, 4 * MINOR, 2 * MINOR))
    eye = np.eye(MINOR)
    conjugate = np.diag(np.concatenate([np.ones(MINOR), -np.ones(MINOR)]))
    for t in range(1, HALF):
        turn = np.exp(2j * math.pi * t / MAJOR)
        out[t, : 2 * MINOR] = as_real((1 + 1j * turn) * np.conj(step[t]).T)
        partner = as_real(np.conj(step[HALF - t]).T)
        out[t, 2 * MINOR :] = partner @ conjugate @ as_real((1 - 1j * turn) * eye)
    half = MINOR // 2
    b = np.arange(MINOR)[None, :]
    s = np.arange(half)[:, None]
    even = 2 * math.pi * (b * s) / MINOR
    odd = 2 * math.pi * (b * (HALF + MAJOR * s)) / LENGTH
    first_re, first_im = 2 * np.cos(even), -2 * np.sin(even)
    first_re[0] = 1.0
    first_im[0] = (-1.0) ** np.arange(MINOR)
    second_re, second_im = 2 * np.cos(odd), -2 * np.sin(odd)
    first = np.concatenate([first_re, 0 * second_re, first_im, 0 * second_im], 0)
    second = np.concatenate([0 * first_re, second_re, 0 * first_im, second_im], 0)
    out[0, : 2 * MINOR] = np.concatenate([first + second, first - second], 1)
    return split_table(out / float(LENGTH * LENGTH))


def add(x, y):
    return (x[0] + y[0], x[1] + y[1])


def sub(x, y):
    return (x[0] - y[0], x[1] - y[1])


def turn(x, index, length):
    index = index % length
    re, im = x
    if index == 0:
        return x
    if 4 * index == length:
        return (im, -re)
    if 2 * index == length:
        return (-re, -im)
    if 4 * index == 3 * length:
        return (-im, re)
    angle = 2.0 * math.pi * index / length
    cosine, sine = math.cos(angle), math.sin(angle)
    if 8 * index == length:
        return ((re + im) * cosine, (im - re) * cosine)
    if 8 * index == 3 * length:
        return ((im - re) * sine, (re + im) * (-sine))
    return (re * cosine + im * sine, im * cosine - re * sine)


def dft4(x):
    a, b = add(x[0], x[2]), sub(x[0], x[2])
    c, d = add(x[1], x[3]), sub(x[1], x[3])
    return [add(a, c), (b[0] + d[1], b[1] - d[0]), sub(a, c), (b[0] - d[1], b[1] + d[0])]


def dft8(x):
    even, odd = dft4(x[0::2]), dft4(x[1::2])
    odd = [turn(value, index, 8) for index, value in enumerate(odd)]
    return [add(e, o) for e, o in zip(even, odd)] + [sub(e, o) for e, o in zip(even, odd)]


def dft16(x):
    middle = [dft4([x[4 * a + b] for a in range(4)]) for b in range(4)]
    out = [None] * 16
    for k in range(4):
        part = dft4([turn(middle[b][k], b * k, 16) for b in range(4)])
        for m in range(4):
            out[k + 4 * m] = part[m]
    return out


def dft4_half(x):
    return [add(x[0], x[1]), (x[0][0] + x[1][1], x[0][1] - x[1][0]), sub(x[0], x[1]), (x[0][0] - x[1][1], x[0][1] + x[1][0])]


def dft32_first(part, b, mid_ref):
    for k in range(4):
        re, im = turn(part[k], b * k, 32)
        mid_ref[2 * (8 * k + b)] = re
        mid_ref[2 * (8 * k + b) + 1] = im


def dft32_last(store, mid_ref):
    for k in range(4):
        part = dft8([(mid_ref[2 * (8 * k + b)], mid_ref[2 * (8 * k + b) + 1]) for b in range(8)])
        for m in range(8):
            store(k + 4 * m, *part[m])


def dft32(load, store, mid_ref):
    for b in range(8):
        dft32_first(dft4([load(8 * a + b) for a in range(4)]), b, mid_ref)
    dft32_last(store, mid_ref)


def dot(x, y):
    return jnp.dot(x, y, preferred_element_type=F32)


def sum_kernel(x_ref, out_ref, total_ref):
    @pl.when(pl.program_id(0) == 0)
    def _():
        total_ref[...] = jnp.zeros_like(total_ref)

    rows = x_ref.shape[2]
    for frame in range(2):
        values = x_ref[0, frame].astype(F32).reshape(rows // 8, 8, LENGTH)
        total_ref[frame] += jnp.sum(values, axis=0)

    @pl.when(pl.program_id(0) == pl.num_programs(0) - 1)
    def _():
        for frame in range(2):
            out_ref[0, frame] = jnp.sum(total_ref[frame])


def frame_sums(intensities):
    rows = intensities.shape[2]
    block = 128
    return pl.pallas_call(
        sum_kernel,
        grid=(rows // block,),
        in_specs=[pl.BlockSpec((1, 2, block, LENGTH), lambda i: (0, 0, i, 0))],
        out_specs=pl.BlockSpec(memory_space=pltpu.SMEM),
        out_shape=jax.ShapeDtypeStruct((1, 2), F32),
        scratch_shapes=[pltpu.VMEM((2, 8, LENGTH), F32)],
        compiler_params=pltpu.CompilerParams(vmem_limit_bytes=58 * MIB),
        name="frame_sums",
    )(intensities)


def row_kernel(chunks, bands, band_ref, scale_ref, x_ref, high_hbm, low_hbm, *rest):
    outs = rest[: chunks * bands]
    mid_ref, xs_ref, high_ref, low_ref, sems = rest[chunks * bands :]
    rows_here = x_ref.shape[2]
    band = band_ref[0]
    scale_even, scale_odd = scale_ref[0, 0], scale_ref[0, 1]

    def fetches():
        return [
            pltpu.make_async_copy(high_hbm, high_ref, sems.at[0]),
            pltpu.make_async_copy(low_hbm, low_ref, sems.at[1]),
        ]

    @pl.when(pl.program_id(0) == 0)
    def _():
        for fetch in fetches():
            fetch.start()

    def group(index, carry):
        rows = pl.ds(pl.multiple_of(index * 16, 16), 16)

        def load(a):
            lanes = slice(MINOR * a, MINOR * (a + 1))
            even = x_ref[0, 0, rows, lanes].astype(F32) * scale_even - 1.0
            odd = x_ref[0, 1, rows, lanes].astype(F32) * scale_odd - 1.0
            return even, odd

        def store(k, re, im):
            for place, value in enumerate((re, im)):
                high = value.astype(BF16)
                low = (value - high.astype(F32)).astype(BF16)
                xs_ref[k, rows, MINOR * place : MINOR * (place + 1)] = high
                xs_ref[k, rows, MINOR * (2 + place) : MINOR * (3 + place)] = low

        dft32(load, store, mid_ref)
        return carry

    lax.fori_loop(0, rows_here // 16, group, 0)

    @pl.when(pl.program_id(0) == 0)
    def _():
        for fetch in fetches():
            fetch.wait()

    def apply(k, table):
        values = xs_ref[k]
        high = high_ref[table]
        whole = jnp.concatenate([values, values[:, : 2 * MINOR]], axis=1)
        return dot(whole, jnp.concatenate([high, high, low_ref[table]], axis=0))

    width = 2 * MINOR
    for chunk in range(chunks):
        for place in range(TILES):
            start = 2 * width * place
            for offset in range(bands):
                t = (chunk * TILES + place) * bands + (band ^ offset)
                out_ref = outs[chunk * bands + offset]
                out_ref[:, start : start + width] = apply(t, 2 * t).astype(BF16)
                out_ref[:, start + width : start + 2 * width] = apply(
                    lax.rem(MAJOR - t, MAJOR), 2 * t + 1
                ).astype(BF16)
    for offset in range(bands):

        @pl.when(band == offset)
        def _(offset=offset):
            outs[offset][:, :width] = (apply(0, 0) + apply(HALF, 32)).astype(BF16)
            outs[offset][:, width : 2 * width] = (apply(0, 1) + apply(HALF, 33)).astype(BF16)


def whole_spec():
    return pl.BlockSpec(memory_space=pltpu.VMEM)


def any_spec():
    return pl.BlockSpec(memory_space=pl.ANY)


def fixed_spec(shape):
    return pl.BlockSpec(shape, lambda *_: (0,) * len(shape), pipeline_mode=pl.Buffered(1))


def rows_forward(intensities, scale, band, bands, chunks):
    rows = intensities.shape[2]
    block = min(256, rows)
    high, low = row_tables()
    width = TILES * 4 * MINOR
    count = chunks * bands
    return pl.pallas_call(
        functools.partial(row_kernel, chunks, bands),
        grid=(rows // block,),
        in_specs=[
            pl.BlockSpec(memory_space=pltpu.SMEM),
            pl.BlockSpec(memory_space=pltpu.SMEM),
            pl.BlockSpec((1, 2, block, LENGTH), lambda i: (0, 0, i, 0)),
            any_spec(),
            any_spec(),
        ],
        out_specs=[pl.BlockSpec((block, width), lambda i: (i, 0))] * count,
        out_shape=[jax.ShapeDtypeStruct((rows, width), BF16)] * count,
        scratch_shapes=[
            pltpu.VMEM((64, 16, MINOR), F32),
            pltpu.VMEM((MAJOR, block, 4 * MINOR), BF16),
            pltpu.VMEM(high.shape, BF16),
            pltpu.VMEM(low.shape, BF16),
            pltpu.SemaphoreType.DMA((2,)),
        ],
        compiler_params=pltpu.CompilerParams(vmem_limit_bytes=58 * MIB),
        cost_estimate=pl.CostEstimate(
            flops=64 * rows * 34 * 6 * 256 * 256, bytes_accessed=4 * rows * LENGTH * 2 + 9 * MIB, transcendentals=0
        ),
        name="rows_forward",
    )(band, scale, intensities, jnp.asarray(high), jnp.asarray(low))


def column_kernel(special, bands, band_ref, v_ref, *rest):
    blocks = rest[:bands]
    u_hbm, *table_hbms = rest[bands : bands + 5]
    rest = rest[bands + 5 :]
    band = band_ref[0]
    if special:
        nyquist_ref, *rest = rest
        lane = lax.broadcasted_iota(jnp.int32, (16, MINOR), 1)
        own = (lane == 0) & (band == 0)
    near_ref, far_ref, mid_ref, xs_ref, ys_ref, x_ref, u_ref, fh_ref, fl_ref, ih_ref, il_ref, sems = rest

    fetches = []
    height = HALF // bands
    for offset in range(bands):
        start = (band ^ offset) * height
        fetches.append(pltpu.make_async_copy(blocks[offset], x_ref.at[pl.ds(start, height)], sems.at[offset]))
    late = []
    for index, (source, target) in enumerate(
        zip([u_hbm] + table_hbms, (u_ref, fh_ref, fl_ref, ih_ref, il_ref))
    ):
        late.append(pltpu.make_async_copy(source, target, sems.at[bands + index]))
    for fetch in fetches + late:
        fetch.start()
    for fetch in fetches:
        fetch.wait()

    def forward(index, carry):
        start = pl.multiple_of(index * 16, 16)
        rows = pl.ds(start, 16)
        below = pl.ds(pl.multiple_of(start + MINOR, 16), 16)
        for tile in range(TILES):
            patch = special and tile == 0

            def load(a, tile=tile, patch=patch):
                pos_re, pos_im, neg_re, neg_im = [
                    x_ref[a, rows, MINOR * i : MINOR * (i + 1)].astype(F32) for i in range(4 * tile, 4 * tile + 4)
                ]
                if patch:
                    neg_re = jnp.where(own, pos_re, neg_re)
                    neg_im = jnp.where(own, pos_im, neg_im)
                return (pos_re + neg_re, pos_im - neg_im), (pos_im + neg_im, neg_re - pos_re)

            for b in range(8):
                values = [load(8 * a + b) for a in range(2)]
                for frame in range(2):
                    part = dft4_half([value[frame] for value in values])
                    dft32_first(part, b, mid_ref.at[2 * tile + frame])
            for frame in range(2):

                def store(k, re, im, tile=tile, frame=frame):
                    lanes = slice(MINOR * (2 * tile + frame), MINOR * (2 * tile + frame + 1))
                    xs_ref[k, rows, lanes] = re.astype(BF16)
                    xs_ref[k, below, lanes] = im.astype(BF16)

                dft32_last(store, mid_ref.at[2 * tile + frame])
        return carry

    lax.fori_loop(0, MINOR // 16, forward, 0)
    for fetch in late:
        fetch.wait()

    along_v = [[v_ref[tile, i : i + 1, :] for i in range(4)] for tile in range(TILES)]

    def middle(k):
        values = xs_ref[k]
        table = jnp.concatenate([fh_ref[k], fl_ref[k]], axis=1)
        spectra = dot(table, jnp.concatenate([values, values], axis=0))
        column = u_ref[k]
        along_u = [column[:, i : i + 1] for i in range(4)]
        parts_re, parts_im = [], []
        for tile in range(TILES):
            sin_even = along_u[0] * along_v[tile][1] + along_u[1] * along_v[tile][0]
            sin_odd = along_u[2] * along_v[tile][3] + along_u[3] * along_v[tile][2]
            scale = 1.0 / (4.0 * (sin_even * sin_even + sin_odd * sin_odd) + 2.0 * alpha_reg)
            sin_even = sin_even * scale
            sin_odd = sin_odd * scale
            even = slice(2 * MINOR * tile, 2 * MINOR * tile + MINOR)
            odd = slice(2 * MINOR * tile + MINOR, 2 * MINOR * (tile + 1))
            phase_re = sin_even * spectra[:MINOR, even] + sin_odd * spectra[:MINOR, odd]
            phase_im = sin_even * spectra[MINOR:, even] + sin_odd * spectra[MINOR:, odd]
            parts_re.append(phase_re.astype(BF16))
            parts_im.append(phase_im.astype(BF16))
        phase = jnp.concatenate([jnp.concatenate(parts_re, axis=1), jnp.concatenate(parts_im, axis=1)], axis=0)
        table = jnp.concatenate([ih_ref[k], il_ref[k]], axis=1)
        ys_ref[k] = dot(table, jnp.concatenate([phase, phase], axis=0))

    def middles(index, carry):
        for step in range(2):
            middle(2 * index + step)
        return carry

    lax.fori_loop(0, MAJOR // 2, middles, 0)

    def inverse(index, carry):
        start = pl.multiple_of(index * 16, 16)
        rows = pl.ds(start, 16)
        below = pl.ds(pl.multiple_of(start + MINOR, 16), 16)
        for tile in range(TILES):
            lanes = slice(MINOR * tile, MINOR * (tile + 1))
            patch = special and tile == 0

            def load(k, lanes=lanes):
                return ys_ref[k, below, lanes], ys_ref[k, rows, lanes]

            def store(a, im, re, tile=tile, patch=patch):
                if patch:
                    im = jnp.where(own, nyquist_ref[rows, a : a + 1], im)
                first = slice(2 * MINOR * tile, 2 * MINOR * tile + MINOR)
                second = slice(2 * MINOR * tile + MINOR, 2 * MINOR * (tile + 1))
                if a < HALF:
                    near_ref[a, rows, first] = re
                    near_ref[a, rows, second] = im
                else:
                    far_ref[a - HALF, rows, first] = re.astype(BF16)
                    far_ref[a - HALF, rows, second] = im.astype(BF16)

            dft32(load, store, mid_ref.at[tile])
        return carry

    lax.fori_loop(0, MINOR // 16, inverse, 0)


def columns(blocks, band, along_u, along_v, nyquist):
    (fh, fl), (ih, il) = column_tables()
    special = nyquist is not None
    bands = len(blocks)
    operands = [band, along_v, *blocks, along_u] + [jnp.asarray(t) for t in (fh, fl, ih, il)]
    in_specs = [pl.BlockSpec(memory_space=pltpu.SMEM), whole_spec()] + [any_spec()] * (bands + 5)
    if special:
        operands.append(nyquist)
        in_specs.append(whole_spec())
    shape = (HALF, MINOR, TILES * 2 * MINOR)
    return pl.pallas_call(
        functools.partial(column_kernel, special, bands),
        in_specs=in_specs,
        out_specs=[whole_spec()] * 2,
        out_shape=[jax.ShapeDtypeStruct(shape, F32), jax.ShapeDtypeStruct(shape, BF16)],
        scratch_shapes=[
            pltpu.VMEM((2 * TILES, 64, 16, MINOR), F32),
            pltpu.VMEM((MAJOR, 2 * MINOR, TILES * 2 * MINOR), BF16),
            pltpu.VMEM((MAJOR, 2 * MINOR, TILES * MINOR), F32),
            pltpu.VMEM((HALF, MINOR, TILES * 4 * MINOR), BF16),
            pltpu.VMEM(along_u.shape, F32),
        ]
        + [pltpu.VMEM(fh.shape, BF16)] * 4
        + [pltpu.SemaphoreType.DMA((bands + 5,))],
        compiler_params=pltpu.CompilerParams(vmem_limit_bytes=58 * MIB),
        cost_estimate=pl.CostEstimate(
            flops=128 * 32 * 8 * 256 * 256 * 256, bytes_accessed=30 * MIB, transcendentals=0
        ),
        name="columns",
    )(*operands)


def final_kernel(chunks, bands, place_ref, *rest):
    ins, (high_ref, low_ref, out_ref, xs_ref, zs_ref) = rest[:chunks], rest[chunks:]
    place = place_ref[...]
    count = place.shape[0]
    width = 2 * MINOR
    for chunk in range(chunks):
        for tile in range(TILES):
            for band in range(bands):
                values = ins[chunk][band, :, :, width * tile : width * (tile + 1)].reshape(count, width)
                xs_ref[(chunk * TILES + tile) * bands + band] = dot(place, values).astype(BF16)

    for t in range(HALF):
        partner = (HALF - t) % HALF
        pair = jnp.concatenate([xs_ref[t], xs_ref[partner]], axis=1)
        pair = jnp.concatenate([pair, pair], axis=1)
        zs_ref[t] = dot(pair, jnp.concatenate([high_ref[t], low_ref[t]], axis=0))

    def group(index, carry):
        for half in range(2):
            rows = pl.ds(pl.multiple_of(index * 16 + 8 * half, 8), 8)
            values = [(zs_ref[t, rows, MINOR:], zs_ref[t, rows, :MINOR]) for t in range(HALF)]
            for n, (odd, even) in enumerate(dft16(values)):
                out_ref[rows, MINOR * 2 * n : MINOR * (2 * n + 1)] = even
                out_ref[rows, MINOR * (2 * n + 1) : MINOR * (2 * n + 2)] = odd
        return carry

    lax.fori_loop(0, count // 16, group, 0)


def rows_inverse(received, proj_order, bands):
    chunks = len(received)
    _, projections, rows, width = received[0].shape
    block = min(256 // projections, rows)
    count = block * projections
    high, low = final_tables()
    to = jnp.arange(count, dtype=jnp.int32)
    slot = proj_order[to // block]
    place = (to[:, None] == ((to % block) * projections + slot)[None, :]).astype(BF16)
    result = pl.pallas_call(
        functools.partial(final_kernel, chunks, bands),
        grid=(rows // block,),
        in_specs=[fixed_spec((count, count))]
        + [pl.BlockSpec((bands, projections, block, width), lambda i: (0, 0, i, 0))] * chunks
        + [fixed_spec(high.shape), fixed_spec(low.shape)],
        out_specs=pl.BlockSpec((count, LENGTH), lambda i: (i, 0)),
        out_shape=jax.ShapeDtypeStruct((rows * projections, LENGTH), F32),
        scratch_shapes=[
            pltpu.VMEM((HALF, count, 2 * MINOR), BF16),
            pltpu.VMEM((HALF, count, 2 * MINOR), F32),
        ],
        compiler_params=pltpu.CompilerParams(vmem_limit_bytes=56 * MIB),
        cost_estimate=pl.CostEstimate(
            flops=rows * projections * 16 * 10 * 256 * 256,
            bytes_accessed=rows * projections * LENGTH * 6 + 8 * MIB,
            transcendentals=0,
        ),
        name="rows_inverse",
    )(place, *received, jnp.asarray(high), jnp.asarray(low))
    return result.reshape(rows, projections, LENGTH)


def folded_square(position, length):
    folded = jnp.minimum(position, length - position).astype(F32) / length
    return folded * folded


def nyquist_column(re, im, coefficient):
    side = 64
    index = np.arange(side)
    angle = 2 * math.pi * np.outer(index, index) / side
    cosine, sine = np.cos(angle), np.sin(angle)
    forward = np.stack([np.stack([cosine, -sine], 1), np.stack([sine, cosine], 1)]).astype(np.float32)
    inverse = np.stack([np.stack([cosine, sine], 1), np.stack([-sine, cosine], 1)]).astype(np.float32)
    twist = 2 * math.pi * np.outer(index, index) / LENGTH
    twist_cos, twist_sin = np.cos(twist).astype(np.float32), np.sin(twist).astype(np.float32)
    contract = functools.partial(jnp.einsum, precision=lax.Precision.HIGHEST, preferred_element_type=F32)
    values = jnp.stack([re, im]).reshape(2, side, side)
    values = contract("cab,cadk->dkb", values, forward)
    values = jnp.stack(
        [values[0] * twist_cos + values[1] * twist_sin, values[1] * twist_cos - values[0] * twist_sin]
    )
    values = contract("ckb,cbdm->dkm", values, forward)
    position = (
        lax.broadcasted_iota(jnp.int32, (side, side), 0) + side * lax.broadcasted_iota(jnp.int32, (side, side), 1)
    )
    freq_sq = folded_square(position, LENGTH) + 0.25
    sines = jnp.sin(math.pi * coefficient[:, None, None] * freq_sq)
    scale = 1.0 / (2.0 * (sines[0] * sines[0] + sines[1] * sines[1]) + alpha_reg)
    values = jnp.stack(
        [
            (sines[0] * values[0] + sines[1] * values[1]) * scale,
            (sines[0] * values[1] - sines[1] * values[0]) * scale,
        ]
    )
    values = contract("ckm,cmdb->dkb", values, inverse)
    values = jnp.stack(
        [values[0] * twist_cos - values[1] * twist_sin, values[1] * twist_cos + values[0] * twist_sin]
    )
    column = contract("ckb,cka->ab", values, inverse[:, :, 0, :])
    return column.reshape(MAJOR, MINOR).T


def on_device(intensities, dist_index, fresnel_table, proj_order):
    rows = intensities.shape[2]
    halves = lax.axis_size("half")
    bands = lax.axis_size("inner")
    projections = lax.axis_size("proj")
    band = lax.axis_index("inner")
    chunks = HALF // (bands * TILES)
    totals = lax.psum(frame_sums(intensities), ("half", "inner"))
    scale = (rows * bands * halves * LENGTH) / totals

    here = jnp.asarray(band, jnp.int32).reshape(1)
    spectra = rows_forward(intensities, scale, here, bands, chunks)

    table_size = fresnel_table.shape[0]
    onehot = (dist_index[0][:, None] == jnp.arange(table_size, dtype=jnp.int32)[None, :]).astype(F32)
    coefficient = jnp.sum(onehot * fresnel_table[None, :], axis=1)
    k_index = lax.broadcasted_iota(jnp.int32, (MAJOR, MINOR), 0)
    s_index = lax.broadcasted_iota(jnp.int32, (MAJOR, MINOR), 1)
    angle_u = math.pi * coefficient[:, None, None] * folded_square(k_index + MAJOR * s_index, LENGTH)
    along_u = jnp.stack([jnp.sin(angle_u[0]), jnp.cos(angle_u[0]), jnp.sin(angle_u[1]), jnp.cos(angle_u[1])], axis=-1)
    tile = jnp.arange(chunks * TILES, dtype=jnp.int32)[:, None] * bands + band
    lane = jnp.arange(MINOR, dtype=jnp.int32)[None, :]
    first_tile = jnp.where(lane < MINOR // 2, MAJOR * lane, HALF + MAJOR * (lane - MINOR // 2))
    position_v = jnp.where(tile == 0, first_tile, tile + MAJOR * lane)
    angle_v = math.pi * coefficient[:, None, None] * folded_square(position_v, LENGTH)
    along_v = jnp.stack([jnp.sin(angle_v[0]), jnp.cos(angle_v[0]), jnp.sin(angle_v[1]), jnp.cos(angle_v[1])], axis=1)

    rows_to = LENGTH // (halves * bands * projections)
    received = []
    for chunk in range(chunks):
        blocks = []
        for offset in range(bands):
            block = spectra[chunk * bands + offset]
            if offset:
                block = lax.ppermute(block, "inner", [(source, source ^ offset) for source in range(bands)])
            blocks.append(block)
        nyquist = None
        if chunk == 0:
            sent = jnp.stack([block[:, 2 * MINOR : 4 * MINOR : MINOR] for block in blocks]).astype(F32)
            sent = sent[jnp.arange(bands, dtype=jnp.int32) ^ band].reshape(bands * rows, 2)
            sent = jnp.pad(sent, ((0, bands * rows), (0, 0)))
            nyquist = nyquist_column(sent[:, 0], sent[:, 1], coefficient)
        blocks = [block.reshape(-1, MINOR, TILES * 4 * MINOR) for block in blocks]
        near, far = columns(blocks, here, along_u, along_v[chunk * TILES : (chunk + 1) * TILES], nyquist)
        from_other = lax.ppermute(far, "half", [(0, 1), (1, 0)])
        phase = (near + from_other.astype(F32)).astype(BF16)
        phase = phase.reshape(bands * projections, rows_to, TILES * 2 * MINOR)
        back = lax.all_to_all(phase, ("inner", "proj"), split_axis=0, concat_axis=0, tiled=True)
        received.append(back.reshape(bands, projections, rows_to, TILES * 2 * MINOR))

    return rows_inverse(received, proj_order, bands)


def solution(mesh):
    proj, band = mesh.devices.shape
    split = jax.sharding.Mesh(mesh.devices.reshape(proj, 2, band // 2), ("proj", "half", "inner"))
    in_specs = (P("proj", None, ("half", "inner"), None), P("proj", None), P(), P())
    out_specs = P(("half", "inner", "proj"), None, None)
    return jax.shard_map(
        on_device, mesh=split, in_specs=in_specs, out_specs=out_specs, check_vma=False
    )
```

```python
import functools
import math

import jax
import jax.numpy as jnp
import numpy as np
from jax import lax
from jax.experimental import pallas as pl
from jax.experimental.pallas import tpu as pltpu
from jax.sharding import PartitionSpec as P

alpha_reg = 0.1
LENGTH = 4096
MAJOR = 32
MINOR = 128
HALF = MAJOR // 2
F32 = jnp.float32
BF16 = jnp.bfloat16
MIB = 1 << 20


def split_table(table):
    high = table.astype(np.float32).astype(jnp.bfloat16)
    low = (table - high.astype(np.float64)).astype(np.float32).astype(jnp.bfloat16)
    return high, low


def as_real(table):
    return np.block([[table.real, table.imag], [-table.imag, table.real]])


@functools.lru_cache(maxsize=None)
def step_tables():
    k = np.arange(MAJOR)[:, None, None]
    b = np.arange(MINOR)[None, :, None]
    s = np.arange(MINOR)[None, None, :]
    return np.exp(-2j * math.pi * ((b * (k + MAJOR * s)) % LENGTH) / LENGTH)


@functools.lru_cache(maxsize=None)
def row_tables():
    step = step_tables()
    out = np.zeros((34, 2 * MINOR, 2 * MINOR))
    for t in range(1, HALF):
        out[2 * t] = as_real(step[t])
        out[2 * t + 1] = as_real(step[MAJOR - t][:, ::-1])
    half = MINOR // 2
    zero = np.zeros((MINOR, half), np.complex128)
    negative = step[0][:, (-np.arange(half)) % MINOR].copy()
    negative[:, 0] = step[0][:, half]
    out[0] = as_real(np.concatenate([step[0][:, :half], zero], 1))
    out[1] = as_real(np.concatenate([negative, zero], 1))
    out[32] = as_real(np.concatenate([zero, step[HALF][:, :half]], 1))
    out[33] = as_real(np.concatenate([zero, step[HALF][:, ::-1][:, :half]], 1))
    return split_table(out)


@functools.lru_cache(maxsize=None)
def column_tables():
    inverse = np.stack([as_real(table) for table in step_tables()])
    return split_table(inverse.transpose(0, 2, 1)), split_table(inverse)


@functools.lru_cache(maxsize=None)
def final_tables():
    step = step_tables()
    out = np.zeros((HALF, 4 * MINOR, 2 * MINOR))
    eye = np.eye(MINOR)
    conjugate = np.diag(np.concatenate([np.ones(MINOR), -np.ones(MINOR)]))
    for t in range(1, HALF):
        turn = np.exp(2j * math.pi * t / MAJOR)
        out[t, : 2 * MINOR] = as_real((1 + 1j * turn) * np.conj(step[t]).T)
        partner = as_real(np.conj(step[HALF - t]).T)
        out[t, 2 * MINOR :] = partner @ conjugate @ as_real((1 - 1j * turn) * eye)
    half = MINOR // 2
    b = np.arange(MINOR)[None, :]
    s = np.arange(half)[:, None]
    even = 2 * math.pi * (b * s) / MINOR
    odd = 2 * math.pi * (b * (HALF + MAJOR * s)) / LENGTH
    first_re, first_im = 2 * np.cos(even), -2 * np.sin(even)
    first_re[0] = 1.0
    first_im[0] = (-1.0) ** np.arange(MINOR)
    second_re, second_im = 2 * np.cos(odd), -2 * np.sin(odd)
    first = np.concatenate([first_re, 0 * second_re, first_im, 0 * second_im], 0)
    second = np.concatenate([0 * first_re, second_re, 0 * first_im, second_im], 0)
    out[0, : 2 * MINOR] = np.concatenate([first + second, first - second], 1)
    return split_table(out / float(LENGTH * LENGTH))


def add(x, y):
    return (x[0] + y[0], x[1] + y[1])


def sub(x, y):
    return (x[0] - y[0], x[1] - y[1])


def turn(x, index, length):
    index = index % length
    re, im = x
    if index == 0:
        return x
    if 4 * index == length:
        return (im, -re)
    if 2 * index == length:
        return (-re, -im)
    if 4 * index == 3 * length:
        return (-im, re)
    angle = 2.0 * math.pi * index / length
    cosine, sine = math.cos(angle), math.sin(angle)
    if 8 * index == length:
        return ((re + im) * cosine, (im - re) * cosine)
    if 8 * index == 3 * length:
        return ((im - re) * sine, (re + im) * (-sine))
    return (re * cosine + im * sine, im * cosine - re * sine)


def dft4(x):
    a, b = add(x[0], x[2]), sub(x[0], x[2])
    c, d = add(x[1], x[3]), sub(x[1], x[3])
    return [add(a, c), (b[0] + d[1], b[1] - d[0]), sub(a, c), (b[0] - d[1], b[1] + d[0])]


def dft8(x):
    even, odd = dft4(x[0::2]), dft4(x[1::2])
    odd = [turn(value, index, 8) for index, value in enumerate(odd)]
    return [add(e, o) for e, o in zip(even, odd)] + [sub(e, o) for e, o in zip(even, odd)]


def dft16(x):
    middle = [dft4([x[4 * a + b] for a in range(4)]) for b in range(4)]
    out = [None] * 16
    for k in range(4):
        part = dft4([turn(middle[b][k], b * k, 16) for b in range(4)])
        for m in range(4):
            out[k + 4 * m] = part[m]
    return out


def dft4_half(x):
    return [add(x[0], x[1]), (x[0][0] + x[1][1], x[0][1] - x[1][0]), sub(x[0], x[1]), (x[0][0] - x[1][1], x[0][1] + x[1][0])]


def dft32_first(part, b, mid_ref):
    for k in range(4):
        re, im = turn(part[k], b * k, 32)
        mid_ref[2 * (8 * k + b)] = re
        mid_ref[2 * (8 * k + b) + 1] = im


def dft32_last(store, mid_ref):
    for k in range(4):
        part = dft8([(mid_ref[2 * (8 * k + b)], mid_ref[2 * (8 * k + b) + 1]) for b in range(8)])
        for m in range(8):
            store(k + 4 * m, *part[m])


def dft32(load, store, mid_ref):
    for b in range(8):
        dft32_first(dft4([load(8 * a + b) for a in range(4)]), b, mid_ref)
    dft32_last(store, mid_ref)


def dot(x, y):
    return jnp.dot(x, y, preferred_element_type=F32)


def sum_kernel(x_ref, out_ref, total_ref):
    @pl.when(pl.program_id(0) == 0)
    def _():
        total_ref[...] = jnp.zeros_like(total_ref)

    rows = x_ref.shape[2]
    for frame in range(2):
        values = x_ref[0, frame].astype(F32).reshape(rows // 8, 8, LENGTH)
        total_ref[frame] += jnp.sum(values, axis=0)

    @pl.when(pl.program_id(0) == pl.num_programs(0) - 1)
    def _():
        for frame in range(2):
            out_ref[0, frame] = jnp.sum(total_ref[frame])


def frame_sums(intensities):
    rows = intensities.shape[2]
    block = 128
    return pl.pallas_call(
        sum_kernel,
        grid=(rows // block,),
        in_specs=[pl.BlockSpec((1, 2, block, LENGTH), lambda i: (0, 0, i, 0))],
        out_specs=pl.BlockSpec(memory_space=pltpu.SMEM),
        out_shape=jax.ShapeDtypeStruct((1, 2), F32),
        scratch_shapes=[pltpu.VMEM((2, 8, LENGTH), F32)],
        compiler_params=pltpu.CompilerParams(vmem_limit_bytes=58 * MIB),
        name="frame_sums",
    )(intensities)


def row_kernel(plan, bands, band_ref, scale_ref, x_ref, high_hbm, low_hbm, *rest):
    outs = rest[: len(plan) * bands]
    mid_ref, xs_ref, high_ref, low_ref, sems = rest[len(plan) * bands :]
    rows_here = x_ref.shape[2]
    band = band_ref[0]
    scale_even, scale_odd = scale_ref[0, 0], scale_ref[0, 1]

    def fetches():
        return [
            pltpu.make_async_copy(high_hbm, high_ref, sems.at[0]),
            pltpu.make_async_copy(low_hbm, low_ref, sems.at[1]),
        ]

    @pl.when(pl.program_id(0) == 0)
    def _():
        for fetch in fetches():
            fetch.start()

    def group(index, carry):
        rows = pl.ds(pl.multiple_of(index * 16, 16), 16)

        def load(a):
            lanes = slice(MINOR * a, MINOR * (a + 1))
            even = x_ref[0, 0, rows, lanes].astype(F32) * scale_even - 1.0
            odd = x_ref[0, 1, rows, lanes].astype(F32) * scale_odd - 1.0
            return even, odd

        def store(k, re, im):
            for place, value in enumerate((re, im)):
                high = value.astype(BF16)
                low = (value - high.astype(F32)).astype(BF16)
                xs_ref[k, rows, MINOR * place : MINOR * (place + 1)] = high
                xs_ref[k, rows, MINOR * (2 + place) : MINOR * (3 + place)] = low

        dft32(load, store, mid_ref)
        return carry

    lax.fori_loop(0, rows_here // 16, group, 0)

    @pl.when(pl.program_id(0) == 0)
    def _():
        for fetch in fetches():
            fetch.wait()

    def apply(k, table):
        values = xs_ref[k]
        high = high_ref[table]
        whole = jnp.concatenate([values, values[:, : 2 * MINOR]], axis=1)
        return dot(whole, jnp.concatenate([high, high, low_ref[table]], axis=0))

    width = 2 * MINOR
    for chunk, slots in enumerate(plan):
        for place, slot in enumerate(slots):
            start = 2 * width * place
            for offset in range(bands):
                t = slot * bands + (band ^ offset)
                out_ref = outs[chunk * bands + offset]
                out_ref[:, start : start + width] = apply(t, 2 * t).astype(BF16)
                out_ref[:, start + width : start + 2 * width] = apply(
                    lax.rem(MAJOR - t, MAJOR), 2 * t + 1
                ).astype(BF16)
    chunk = special_chunk(plan)
    for offset in range(bands):

        @pl.when(band == offset)
        def _(out_ref=outs[chunk * bands + offset]):
            out_ref[:, :width] = (apply(0, 0) + apply(HALF, 32)).astype(BF16)
            out_ref[:, width : 2 * width] = (apply(0, 1) + apply(HALF, 33)).astype(BF16)


def chunk_plan(count):
    if count < 4:
        return [[slot] for slot in range(1, count)] + [[0]]
    order = [1, 2, 3, 0] + list(range(4, count))
    return [order[:1]] + [order[i : i + 2] for i in range(1, count - 1, 2)] + [order[count - 1 :]]


def special_chunk(plan):
    return next(chunk for chunk, slots in enumerate(plan) if slots[0] == 0)


def whole_spec():
    return pl.BlockSpec(memory_space=pltpu.VMEM)


def any_spec():
    return pl.BlockSpec(memory_space=pl.ANY)


def fixed_spec(shape):
    return pl.BlockSpec(shape, lambda *_: (0,) * len(shape), pipeline_mode=pl.Buffered(1))


def rows_forward(intensities, scale, band, bands, plan):
    rows = intensities.shape[2]
    block = min(256, rows)
    high, low = row_tables()
    widths = [len(slots) * 4 * MINOR for slots in plan for _ in range(bands)]
    return pl.pallas_call(
        functools.partial(row_kernel, plan, bands),
        grid=(rows // block,),
        in_specs=[
            pl.BlockSpec(memory_space=pltpu.SMEM),
            pl.BlockSpec(memory_space=pltpu.SMEM),
            pl.BlockSpec((1, 2, block, LENGTH), lambda i: (0, 0, i, 0)),
            any_spec(),
            any_spec(),
        ],
        out_specs=[pl.BlockSpec((block, width), lambda i: (i, 0)) for width in widths],
        out_shape=[jax.ShapeDtypeStruct((rows, width), BF16) for width in widths],
        scratch_shapes=[
            pltpu.VMEM((64, 16, MINOR), F32),
            pltpu.VMEM((MAJOR, block, 4 * MINOR), BF16),
            pltpu.VMEM(high.shape, BF16),
            pltpu.VMEM(low.shape, BF16),
            pltpu.SemaphoreType.DMA((2,)),
        ],
        compiler_params=pltpu.CompilerParams(vmem_limit_bytes=58 * MIB),
        cost_estimate=pl.CostEstimate(
            flops=64 * rows * 34 * 6 * 256 * 256, bytes_accessed=4 * rows * LENGTH * 2 + 9 * MIB, transcendentals=0
        ),
        name="rows_forward",
    )(band, scale, intensities, jnp.asarray(high), jnp.asarray(low))


def column_kernel(special, tiles, bands, waits, band_ref, v_ref, *rest):
    blocks = rest[:bands]
    u_hbm, *table_hbms = rest[bands : bands + 5]
    rest = rest[bands + 5 + waits :]
    band = band_ref[0]
    if special:
        nyquist_ref, *rest = rest
        lane = lax.broadcasted_iota(jnp.int32, (16, MINOR), 1)
        own = (lane == 0) & (band == 0)
    near_ref, far_ref, mid_ref, xs_ref, ys_ref, x_ref, u_ref, fh_ref, fl_ref, ih_ref, il_ref, sems = rest

    fetches = []
    height = HALF // bands
    for offset in range(bands):
        start = (band ^ offset) * height
        fetches.append(pltpu.make_async_copy(blocks[offset], x_ref.at[pl.ds(start, height)], sems.at[offset]))
    late = []
    for index, (source, target) in enumerate(
        zip([u_hbm] + table_hbms, (u_ref, fh_ref, fl_ref, ih_ref, il_ref))
    ):
        late.append(pltpu.make_async_copy(source, target, sems.at[bands + index]))
    for fetch in fetches + late:
        fetch.start()
    for fetch in fetches:
        fetch.wait()

    def forward(index, carry):
        start = pl.multiple_of(index * 16, 16)
        rows = pl.ds(start, 16)
        below = pl.ds(pl.multiple_of(start + MINOR, 16), 16)
        for tile in range(tiles):
            patch = special and tile == 0

            def load(a, tile=tile, patch=patch):
                pos_re, pos_im, neg_re, neg_im = [
                    x_ref[a, rows, MINOR * i : MINOR * (i + 1)].astype(F32) for i in range(4 * tile, 4 * tile + 4)
                ]
                if patch:
                    neg_re = jnp.where(own, pos_re, neg_re)
                    neg_im = jnp.where(own, pos_im, neg_im)
                return (pos_re + neg_re, pos_im - neg_im), (pos_im + neg_im, neg_re - pos_re)

            for b in range(8):
                values = [load(8 * a + b) for a in range(2)]
                for frame in range(2):
                    part = dft4_half([value[frame] for value in values])
                    dft32_first(part, b, mid_ref.at[2 * tile + frame])
            for frame in range(2):

                def store(k, re, im, tile=tile, frame=frame):
                    lanes = slice(MINOR * (2 * tile + frame), MINOR * (2 * tile + frame + 1))
                    xs_ref[k, rows, lanes] = re.astype(BF16)
                    xs_ref[k, below, lanes] = im.astype(BF16)

                dft32_last(store, mid_ref.at[2 * tile + frame])
        return carry

    lax.fori_loop(0, MINOR // 16, forward, 0)
    for fetch in late:
        fetch.wait()

    along_v = [[v_ref[tile, i : i + 1, :] for i in range(4)] for tile in range(tiles)]

    def middle(k):
        values = xs_ref[k]
        table = jnp.concatenate([fh_ref[k], fl_ref[k]], axis=1)
        spectra = dot(table, jnp.concatenate([values, values], axis=0))
        column = u_ref[k]
        along_u = [column[:, i : i + 1] for i in range(4)]
        parts_re, parts_im = [], []
        for tile in range(tiles):
            sin_even = along_u[0] * along_v[tile][1] + along_u[1] * along_v[tile][0]
            sin_odd = along_u[2] * along_v[tile][3] + along_u[3] * along_v[tile][2]
            scale = 1.0 / (4.0 * (sin_even * sin_even + sin_odd * sin_odd) + 2.0 * alpha_reg)
            sin_even = sin_even * scale
            sin_odd = sin_odd * scale
            even = slice(2 * MINOR * tile, 2 * MINOR * tile + MINOR)
            odd = slice(2 * MINOR * tile + MINOR, 2 * MINOR * (tile + 1))
            phase_re = sin_even * spectra[:MINOR, even] + sin_odd * spectra[:MINOR, odd]
            phase_im = sin_even * spectra[MINOR:, even] + sin_odd * spectra[MINOR:, odd]
            parts_re.append(phase_re.astype(BF16))
            parts_im.append(phase_im.astype(BF16))
        phase = jnp.concatenate([jnp.concatenate(parts_re, axis=1), jnp.concatenate(parts_im, axis=1)], axis=0)
        table = jnp.concatenate([ih_ref[k], il_ref[k]], axis=1)
        ys_ref[k] = dot(table, jnp.concatenate([phase, phase], axis=0))

    def middles(index, carry):
        for step in range(2):
            middle(2 * index + step)
        return carry

    lax.fori_loop(0, MAJOR // 2, middles, 0)

    def inverse(index, carry):
        start = pl.multiple_of(index * 16, 16)
        rows = pl.ds(start, 16)
        below = pl.ds(pl.multiple_of(start + MINOR, 16), 16)
        for tile in range(tiles):
            lanes = slice(MINOR * tile, MINOR * (tile + 1))
            patch = special and tile == 0

            def load(k, lanes=lanes):
                return ys_ref[k, below, lanes], ys_ref[k, rows, lanes]

            def store(a, im, re, tile=tile, patch=patch):
                if patch:
                    im = jnp.where(own, nyquist_ref[rows, a : a + 1], im)
                first = slice(2 * MINOR * tile, 2 * MINOR * tile + MINOR)
                second = slice(2 * MINOR * tile + MINOR, 2 * MINOR * (tile + 1))
                if a < HALF:
                    near_ref[a, rows, first] = re
                    near_ref[a, rows, second] = im
                else:
                    far_ref[a - HALF, rows, first] = re.astype(BF16)
                    far_ref[a - HALF, rows, second] = im.astype(BF16)

            dft32(load, store, mid_ref.at[tile])
        return carry

    lax.fori_loop(0, MINOR // 16, inverse, 0)


def columns(blocks, band, along_u, along_v, nyquist, after):
    tiles = along_v.shape[0]
    (fh, fl), (ih, il) = column_tables()
    special = nyquist is not None
    bands = len(blocks)
    operands = [band, along_v, *blocks, along_u] + [jnp.asarray(t) for t in (fh, fl, ih, il)] + after
    in_specs = [pl.BlockSpec(memory_space=pltpu.SMEM), whole_spec()] + [any_spec()] * (bands + 5 + len(after))
    if special:
        operands.append(nyquist)
        in_specs.append(whole_spec())
    shape = (HALF, MINOR, tiles * 2 * MINOR)
    return pl.pallas_call(
        functools.partial(column_kernel, special, tiles, bands, len(after)),
        in_specs=in_specs,
        out_specs=[whole_spec()] * 2,
        out_shape=[jax.ShapeDtypeStruct(shape, F32), jax.ShapeDtypeStruct(shape, BF16)],
        scratch_shapes=[
            pltpu.VMEM((2 * tiles, 64, 16, MINOR), F32),
            pltpu.VMEM((MAJOR, 2 * MINOR, tiles * 2 * MINOR), BF16),
            pltpu.VMEM((MAJOR, 2 * MINOR, tiles * MINOR), F32),
            pltpu.VMEM((HALF, MINOR, tiles * 4 * MINOR), BF16),
            pltpu.VMEM(along_u.shape, F32),
        ]
        + [pltpu.VMEM(fh.shape, BF16)] * 4
        + [pltpu.SemaphoreType.DMA((bands + 5,))],
        compiler_params=pltpu.CompilerParams(vmem_limit_bytes=58 * MIB),
        cost_estimate=pl.CostEstimate(
            flops=tiles * 64 * 32 * 8 * 256 * 256 * 256, bytes_accessed=30 * MIB, transcendentals=0
        ),
        name="columns",
    )(*operands)


def share_kernel(near_ref, far_ref, *rest):
    rest[-1][...] = (near_ref[...] + far_ref[...].astype(F32)).astype(BF16)


def add_shares(near, far, after):
    block = (4,) + near.shape[1:]
    spec = pl.BlockSpec(block, lambda i: (i, 0, 0))
    return pl.pallas_call(
        share_kernel,
        grid=(near.shape[0] // 4,),
        in_specs=[spec, spec] + [any_spec()] * len(after),
        out_specs=spec,
        out_shape=jax.ShapeDtypeStruct(near.shape, BF16),
        compiler_params=pltpu.CompilerParams(vmem_limit_bytes=58 * MIB),
        name="add_shares",
    )(near, far, *after)


def final_kernel(plan, bands, place_ref, *rest):
    ins, (high_ref, low_ref, out_ref, xs_ref, zs_ref) = rest[: len(plan)], rest[len(plan) :]
    place = place_ref[...]
    count = place.shape[0]
    width = 2 * MINOR
    for chunk, slots in enumerate(plan):
        for tile, slot in enumerate(slots):
            for band in range(bands):
                values = ins[chunk][band, :, :, width * tile : width * (tile + 1)].reshape(count, width)
                xs_ref[slot * bands + band] = dot(place, values).astype(BF16)

    for t in range(HALF):
        partner = (HALF - t) % HALF
        pair = jnp.concatenate([xs_ref[t], xs_ref[partner]], axis=1)
        pair = jnp.concatenate([pair, pair], axis=1)
        zs_ref[t] = dot(pair, jnp.concatenate([high_ref[t], low_ref[t]], axis=0))

    def group(index, carry):
        for half in range(2):
            rows = pl.ds(pl.multiple_of(index * 16 + 8 * half, 8), 8)
            values = [(zs_ref[t, rows, MINOR:], zs_ref[t, rows, :MINOR]) for t in range(HALF)]
            for n, (odd, even) in enumerate(dft16(values)):
                out_ref[rows, MINOR * 2 * n : MINOR * (2 * n + 1)] = even
                out_ref[rows, MINOR * (2 * n + 1) : MINOR * (2 * n + 2)] = odd
        return carry

    lax.fori_loop(0, count // 16, group, 0)


def rows_inverse(received, proj_order, bands, plan):
    _, projections, rows, _ = received[0].shape
    block = min(256 // projections, rows)
    count = block * projections
    high, low = final_tables()
    to = jnp.arange(count, dtype=jnp.int32)
    slot = proj_order[to // block]
    place = (to[:, None] == ((to % block) * projections + slot)[None, :]).astype(BF16)
    result = pl.pallas_call(
        functools.partial(final_kernel, plan, bands),
        grid=(rows // block,),
        in_specs=[fixed_spec((count, count))]
        + [pl.BlockSpec((bands, projections, block, each.shape[3]), lambda i: (0, 0, i, 0)) for each in received]
        + [fixed_spec(high.shape), fixed_spec(low.shape)],
        out_specs=pl.BlockSpec((count, LENGTH), lambda i: (i, 0)),
        out_shape=jax.ShapeDtypeStruct((rows * projections, LENGTH), F32),
        scratch_shapes=[
            pltpu.VMEM((HALF, count, 2 * MINOR), BF16),
            pltpu.VMEM((HALF, count, 2 * MINOR), F32),
        ],
        compiler_params=pltpu.CompilerParams(vmem_limit_bytes=56 * MIB),
        cost_estimate=pl.CostEstimate(
            flops=rows * projections * 16 * 10 * 256 * 256,
            bytes_accessed=rows * projections * LENGTH * 6 + 8 * MIB,
            transcendentals=0,
        ),
        name="rows_inverse",
    )(place, *received, jnp.asarray(high), jnp.asarray(low))
    return result.reshape(rows, projections, LENGTH)


def folded_square(position, length):
    folded = jnp.minimum(position, length - position).astype(F32) / length
    return folded * folded


def nyquist_column(re, im, coefficient):
    side = 64
    index = np.arange(side)
    angle = 2 * math.pi * np.outer(index, index) / side
    cosine, sine = np.cos(angle), np.sin(angle)
    forward = np.stack([np.stack([cosine, -sine], 1), np.stack([sine, cosine], 1)]).astype(np.float32)
    inverse = np.stack([np.stack([cosine, sine], 1), np.stack([-sine, cosine], 1)]).astype(np.float32)
    twist = 2 * math.pi * np.outer(index, index) / LENGTH
    twist_cos, twist_sin = np.cos(twist).astype(np.float32), np.sin(twist).astype(np.float32)
    contract = functools.partial(jnp.einsum, precision=lax.Precision.HIGHEST, preferred_element_type=F32)
    values = jnp.stack([re, im]).reshape(2, side, side)
    values = contract("cab,cadk->dkb", values, forward)
    values = jnp.stack(
        [values[0] * twist_cos + values[1] * twist_sin, values[1] * twist_cos - values[0] * twist_sin]
    )
    values = contract("ckb,cbdm->dkm", values, forward)
    position = (
        lax.broadcasted_iota(jnp.int32, (side, side), 0) + side * lax.broadcasted_iota(jnp.int32, (side, side), 1)
    )
    freq_sq = folded_square(position, LENGTH) + 0.25
    sines = jnp.sin(math.pi * coefficient[:, None, None] * freq_sq)
    scale = 1.0 / (2.0 * (sines[0] * sines[0] + sines[1] * sines[1]) + alpha_reg)
    values = jnp.stack(
        [
            (sines[0] * values[0] + sines[1] * values[1]) * scale,
            (sines[0] * values[1] - sines[1] * values[0]) * scale,
        ]
    )
    values = contract("ckm,cmdb->dkb", values, inverse)
    values = jnp.stack(
        [values[0] * twist_cos - values[1] * twist_sin, values[1] * twist_cos + values[0] * twist_sin]
    )
    column = contract("ckb,cka->ab", values, inverse[:, :, 0, :])
    return column.reshape(MAJOR, MINOR).T


def on_device(intensities, dist_index, fresnel_table, proj_order):
    rows = intensities.shape[2]
    halves = lax.axis_size("half")
    bands = lax.axis_size("inner")
    projections = lax.axis_size("proj")
    band = lax.axis_index("inner")
    slots = HALF // bands
    plan = chunk_plan(slots)
    totals = lax.psum(frame_sums(intensities), ("half", "inner"))
    scale = (rows * bands * halves * LENGTH) / totals

    here = jnp.asarray(band, jnp.int32).reshape(1)
    spectra = rows_forward(intensities, scale, here, bands, plan)

    table_size = fresnel_table.shape[0]
    onehot = (dist_index[0][:, None] == jnp.arange(table_size, dtype=jnp.int32)[None, :]).astype(F32)
    coefficient = jnp.sum(onehot * fresnel_table[None, :], axis=1)
    k_index = lax.broadcasted_iota(jnp.int32, (MAJOR, MINOR), 0)
    s_index = lax.broadcasted_iota(jnp.int32, (MAJOR, MINOR), 1)
    angle_u = math.pi * coefficient[:, None, None] * folded_square(k_index + MAJOR * s_index, LENGTH)
    along_u = jnp.stack([jnp.sin(angle_u[0]), jnp.cos(angle_u[0]), jnp.sin(angle_u[1]), jnp.cos(angle_u[1])], axis=-1)
    tile = jnp.asarray(sum(plan, []), jnp.int32)[:, None] * bands + band
    lane = jnp.arange(MINOR, dtype=jnp.int32)[None, :]
    first_tile = jnp.where(lane < MINOR // 2, MAJOR * lane, HALF + MAJOR * (lane - MINOR // 2))
    position_v = jnp.where(tile == 0, first_tile, tile + MAJOR * lane)
    angle_v = math.pi * coefficient[:, None, None] * folded_square(position_v, LENGTH)
    along_v = jnp.stack([jnp.sin(angle_v[0]), jnp.cos(angle_v[0]), jnp.sin(angle_v[1]), jnp.cos(angle_v[1])], axis=1)

    rows_to = LENGTH // (halves * bands * projections)
    phases, pending, after = [], [], []
    for chunk, members in enumerate(plan):
        blocks = []
        for offset in range(bands):
            block = spectra[chunk * bands + offset]
            if offset:
                block = lax.ppermute(block, "inner", [(source, source ^ offset) for source in range(bands)])
            blocks.append(block)
        nyquist = None
        if chunk == special_chunk(plan):
            sent = jnp.stack([block[:, 2 * MINOR : 4 * MINOR : MINOR] for block in blocks]).astype(F32)
            sent = sent[jnp.arange(bands, dtype=jnp.int32) ^ band].reshape(bands * rows, 2)
            sent = jnp.pad(sent, ((0, bands * rows), (0, 0)))
            nyquist = nyquist_column(sent[:, 0], sent[:, 1], coefficient)
        width = len(members) * 4 * MINOR
        start = sum(len(each) for each in plan[:chunk])
        blocks = [block.reshape(-1, MINOR, width) for block in blocks]
        near, far = columns(blocks, here, along_u, along_v[start : start + len(members)], nyquist, after)
        if pending:
            phases.append(add_shares(*pending.pop(), [far]))
        pending.append((near, lax.ppermute(far, "half", [(0, 1), (1, 0)])))
        after = [far] if chunk == 0 else [phases[-1]]
    phases.append(add_shares(*pending.pop(), []))

    received = []
    for phase in phases:
        phase = phase.reshape(bands * projections, rows_to, phase.shape[2])
        back = lax.all_to_all(phase, ("inner", "proj"), split_axis=0, concat_axis=0, tiled=True)
        received.append(back.reshape(bands, projections, rows_to, phase.shape[2]))

    return rows_inverse(received, proj_order, bands, plan)


def solution(mesh):
    proj, band = mesh.devices.shape
    split = jax.sharding.Mesh(mesh.devices.reshape(proj, 2, band // 2), ("proj", "half", "inner"))
    in_specs = (P("proj", None, ("half", "inner"), None), P("proj", None), P(), P())
    out_specs = P(("half", "inner", "proj"), None, None)
    return jax.shard_map(
        on_device, mesh=split, in_specs=in_specs, out_specs=out_specs, check_vma=False
    )
```

```python
import functools
import math

import jax
import jax.numpy as jnp
import numpy as np
from jax import lax
from jax.experimental import pallas as pl
from jax.experimental.pallas import tpu as pltpu
from jax.sharding import PartitionSpec as P

alpha_reg = 0.1
LENGTH = 4096
MAJOR = 32
MINOR = 128
HALF = MAJOR // 2
F32 = jnp.float32
BF16 = jnp.bfloat16
MIB = 1 << 20


def split_table(table):
    high = table.astype(np.float32).astype(jnp.bfloat16)
    low = (table - high.astype(np.float64)).astype(np.float32).astype(jnp.bfloat16)
    return high, low


def as_real(table):
    return np.block([[table.real, table.imag], [-table.imag, table.real]])


@functools.lru_cache(maxsize=None)
def step_tables():
    k = np.arange(MAJOR)[:, None, None]
    b = np.arange(MINOR)[None, :, None]
    s = np.arange(MINOR)[None, None, :]
    return np.exp(-2j * math.pi * ((b * (k + MAJOR * s)) % LENGTH) / LENGTH)


@functools.lru_cache(maxsize=None)
def row_tables():
    step = step_tables()
    out = np.zeros((34, 2 * MINOR, 2 * MINOR))
    for t in range(1, HALF):
        out[2 * t] = as_real(step[t])
        out[2 * t + 1] = as_real(step[MAJOR - t][:, ::-1])
    half = MINOR // 2
    zero = np.zeros((MINOR, half), np.complex128)
    negative = step[0][:, (-np.arange(half)) % MINOR].copy()
    negative[:, 0] = step[0][:, half]
    out[0] = as_real(np.concatenate([step[0][:, :half], zero], 1))
    out[1] = as_real(np.concatenate([negative, zero], 1))
    out[32] = as_real(np.concatenate([zero, step[HALF][:, :half]], 1))
    out[33] = as_real(np.concatenate([zero, step[HALF][:, ::-1][:, :half]], 1))
    return split_table(out)


@functools.lru_cache(maxsize=None)
def column_tables():
    inverse = np.stack([as_real(table) for table in step_tables()])
    return split_table(inverse.transpose(0, 2, 1)), split_table(inverse)


@functools.lru_cache(maxsize=None)
def final_tables():
    step = step_tables()
    out = np.zeros((HALF, 4 * MINOR, 2 * MINOR))
    eye = np.eye(MINOR)
    conjugate = np.diag(np.concatenate([np.ones(MINOR), -np.ones(MINOR)]))
    for t in range(1, HALF):
        turn = np.exp(2j * math.pi * t / MAJOR)
        out[t, : 2 * MINOR] = as_real((1 + 1j * turn) * np.conj(step[t]).T)
        partner = as_real(np.conj(step[HALF - t]).T)
        out[t, 2 * MINOR :] = partner @ conjugate @ as_real((1 - 1j * turn) * eye)
    half = MINOR // 2
    b = np.arange(MINOR)[None, :]
    s = np.arange(half)[:, None]
    even = 2 * math.pi * (b * s) / MINOR
    odd = 2 * math.pi * (b * (HALF + MAJOR * s)) / LENGTH
    first_re, first_im = 2 * np.cos(even), -2 * np.sin(even)
    first_re[0] = 1.0
    first_im[0] = (-1.0) ** np.arange(MINOR)
    second_re, second_im = 2 * np.cos(odd), -2 * np.sin(odd)
    first = np.concatenate([first_re, 0 * second_re, first_im, 0 * second_im], 0)
    second = np.concatenate([0 * first_re, second_re, 0 * first_im, second_im], 0)
    out[0, : 2 * MINOR] = np.concatenate([first + second, first - second], 1)
    return split_table(out / float(LENGTH * LENGTH))


def add(x, y):
    return (x[0] + y[0], x[1] + y[1])


def sub(x, y):
    return (x[0] - y[0], x[1] - y[1])


def turn(x, index, length):
    index = index % length
    re, im = x
    if index == 0:
        return x
    if 4 * index == length:
        return (im, -re)
    if 2 * index == length:
        return (-re, -im)
    if 4 * index == 3 * length:
        return (-im, re)
    angle = 2.0 * math.pi * index / length
    cosine, sine = math.cos(angle), math.sin(angle)
    if 8 * index == length:
        return ((re + im) * cosine, (im - re) * cosine)
    if 8 * index == 3 * length:
        return ((im - re) * sine, (re + im) * (-sine))
    return (re * cosine + im * sine, im * cosine - re * sine)


def dft4(x):
    a, b = add(x[0], x[2]), sub(x[0], x[2])
    c, d = add(x[1], x[3]), sub(x[1], x[3])
    return [add(a, c), (b[0] + d[1], b[1] - d[0]), sub(a, c), (b[0] - d[1], b[1] + d[0])]


def dft8(x):
    even, odd = dft4(x[0::2]), dft4(x[1::2])
    odd = [turn(value, index, 8) for index, value in enumerate(odd)]
    return [add(e, o) for e, o in zip(even, odd)] + [sub(e, o) for e, o in zip(even, odd)]


def dft16(x):
    middle = [dft4([x[4 * a + b] for a in range(4)]) for b in range(4)]
    out = [None] * 16
    for k in range(4):
        part = dft4([turn(middle[b][k], b * k, 16) for b in range(4)])
        for m in range(4):
            out[k + 4 * m] = part[m]
    return out


def dft4_half(x):
    return [add(x[0], x[1]), (x[0][0] + x[1][1], x[0][1] - x[1][0]), sub(x[0], x[1]), (x[0][0] - x[1][1], x[0][1] + x[1][0])]


def dft32_first(part, b, mid_ref):
    for k in range(4):
        re, im = turn(part[k], b * k, 32)
        mid_ref[2 * (8 * k + b)] = re
        mid_ref[2 * (8 * k + b) + 1] = im


def dft32_last(store, mid_ref):
    for k in range(4):
        part = dft8([(mid_ref[2 * (8 * k + b)], mid_ref[2 * (8 * k + b) + 1]) for b in range(8)])
        for m in range(8):
            store(k + 4 * m, *part[m])


def dft32(load, store, mid_ref):
    for b in range(8):
        dft32_first(dft4([load(8 * a + b) for a in range(4)]), b, mid_ref)
    dft32_last(store, mid_ref)


def dot(x, y):
    return jnp.dot(x, y, preferred_element_type=F32)


def sum_kernel(x_ref, out_ref, total_ref):
    @pl.when(pl.program_id(0) == 0)
    def _():
        total_ref[...] = jnp.zeros_like(total_ref)

    rows = x_ref.shape[2]
    for frame in range(2):
        for start in range(0, LENGTH, 8 * MINOR):
            lanes = slice(start, start + 8 * MINOR)
            total = total_ref[frame, :, lanes]
            for row in range(0, rows, 16):
                values = x_ref[0, frame, row : row + 16, lanes].astype(F32)
                total = total + (values[:8] + values[8:])
            total_ref[frame, :, lanes] = total

    @pl.when(pl.program_id(0) == pl.num_programs(0) - 1)
    def _():
        for frame in range(2):
            out_ref[0, frame] = jnp.sum(total_ref[frame])


def frame_sums(intensities):
    rows = intensities.shape[2]
    block = 128
    return pl.pallas_call(
        sum_kernel,
        grid=(rows // block,),
        in_specs=[pl.BlockSpec((1, 2, block, LENGTH), lambda i: (0, 0, i, 0))],
        out_specs=pl.BlockSpec(memory_space=pltpu.SMEM),
        out_shape=jax.ShapeDtypeStruct((1, 2), F32),
        scratch_shapes=[pltpu.VMEM((2, 8, LENGTH), F32)],
        compiler_params=pltpu.CompilerParams(vmem_limit_bytes=58 * MIB),
        name="frame_sums",
    )(intensities)


def row_kernel(plan, bands, band_ref, scale_ref, x_ref, high_hbm, low_hbm, *rest):
    outs = rest[: len(plan) * bands]
    mid_ref, xs_ref, high_ref, low_ref, sems = rest[len(plan) * bands :]
    rows_here = x_ref.shape[2]
    band = band_ref[0]
    scale_even, scale_odd = scale_ref[0, 0], scale_ref[0, 1]

    def fetches():
        return [
            pltpu.make_async_copy(high_hbm, high_ref, sems.at[0]),
            pltpu.make_async_copy(low_hbm, low_ref, sems.at[1]),
        ]

    @pl.when(pl.program_id(0) == 0)
    def _():
        for fetch in fetches():
            fetch.start()

    def group(index, carry):
        rows = pl.ds(pl.multiple_of(index * 16, 16), 16)

        def load(a):
            lanes = slice(MINOR * a, MINOR * (a + 1))
            even = x_ref[0, 0, rows, lanes].astype(F32) * scale_even - 1.0
            odd = x_ref[0, 1, rows, lanes].astype(F32) * scale_odd - 1.0
            return even, odd

        def store(k, re, im):
            for place, value in enumerate((re, im)):
                high = value.astype(BF16)
                low = (value - high.astype(F32)).astype(BF16)
                xs_ref[k, rows, MINOR * place : MINOR * (place + 1)] = high
                xs_ref[k, rows, MINOR * (2 + place) : MINOR * (3 + place)] = low

        dft32(load, store, mid_ref)
        return carry

    lax.fori_loop(0, rows_here // 16, group, 0)

    @pl.when(pl.program_id(0) == 0)
    def _():
        for fetch in fetches():
            fetch.wait()

    def apply(k, table):
        values = xs_ref[k]
        high = high_ref[table]
        whole = jnp.concatenate([values, values[:, : 2 * MINOR]], axis=1)
        return dot(whole, jnp.concatenate([high, high, low_ref[table]], axis=0))

    width = 2 * MINOR
    for chunk, slots in enumerate(plan):
        for place, slot in enumerate(slots):
            start = 2 * width * place
            for offset in range(bands):
                t = slot * bands + (band ^ offset)
                out_ref = outs[chunk * bands + offset]
                out_ref[:, start : start + width] = apply(t, 2 * t).astype(BF16)
                out_ref[:, start + width : start + 2 * width] = apply(
                    lax.rem(MAJOR - t, MAJOR), 2 * t + 1
                ).astype(BF16)
    chunk = special_chunk(plan)
    for offset in range(bands):

        @pl.when(band == offset)
        def _(out_ref=outs[chunk * bands + offset]):
            out_ref[:, :width] = (apply(0, 0) + apply(HALF, 32)).astype(BF16)
            out_ref[:, width : 2 * width] = (apply(0, 1) + apply(HALF, 33)).astype(BF16)


def chunk_plan(count):
    if count < 8:
        return [[slot] for slot in range(1, count)] + [[0]]
    order = [1, 2, 3, 4, 0] + list(range(5, count))
    return [order[i : i + 2] for i in range(0, count, 2)]


def special_chunk(plan):
    return next(chunk for chunk, slots in enumerate(plan) if slots[0] == 0)


def whole_spec():
    return pl.BlockSpec(memory_space=pltpu.VMEM)


def any_spec():
    return pl.BlockSpec(memory_space=pl.ANY)


def fixed_spec(shape):
    return pl.BlockSpec(shape, lambda *_: (0,) * len(shape), pipeline_mode=pl.Buffered(1))


def rows_forward(intensities, scale, band, bands, plan):
    rows = intensities.shape[2]
    block = min(256, rows)
    high, low = row_tables()
    widths = [len(slots) * 4 * MINOR for slots in plan for _ in range(bands)]
    return pl.pallas_call(
        functools.partial(row_kernel, plan, bands),
        grid=(rows // block,),
        in_specs=[
            pl.BlockSpec(memory_space=pltpu.SMEM),
            pl.BlockSpec(memory_space=pltpu.SMEM),
            pl.BlockSpec((1, 2, block, LENGTH), lambda i: (0, 0, i, 0)),
            any_spec(),
            any_spec(),
        ],
        out_specs=[pl.BlockSpec((block, width), lambda i: (i, 0)) for width in widths],
        out_shape=[jax.ShapeDtypeStruct((rows, width), BF16) for width in widths],
        scratch_shapes=[
            pltpu.VMEM((64, 16, MINOR), F32),
            pltpu.VMEM((MAJOR, block, 4 * MINOR), BF16),
            pltpu.VMEM(high.shape, BF16),
            pltpu.VMEM(low.shape, BF16),
            pltpu.SemaphoreType.DMA((2,)),
        ],
        compiler_params=pltpu.CompilerParams(vmem_limit_bytes=58 * MIB),
        cost_estimate=pl.CostEstimate(
            flops=64 * rows * 34 * 6 * 256 * 256, bytes_accessed=4 * rows * LENGTH * 2 + 9 * MIB, transcendentals=0
        ),
        name="rows_forward",
    )(band, scale, intensities, jnp.asarray(high), jnp.asarray(low))


def column_kernel(special, tiles, bands, waits, band_ref, v_ref, *rest):
    blocks = rest[:bands]
    u_hbm, *table_hbms = rest[bands : bands + 5]
    rest = rest[bands + 5 + waits :]
    band = band_ref[0]
    if special:
        nyquist_ref, *rest = rest
        lane = lax.broadcasted_iota(jnp.int32, (16, MINOR), 1)
        own = (lane == 0) & (band == 0)
    near_ref, far_ref, mid_ref, xs_ref, ys_ref, x_ref, u_ref, fh_ref, fl_ref, ih_ref, il_ref, sems = rest

    fetches = []
    height = HALF // bands
    for offset in range(bands):
        start = (band ^ offset) * height
        fetches.append(pltpu.make_async_copy(blocks[offset], x_ref.at[pl.ds(start, height)], sems.at[offset]))
    late = []
    for index, (source, target) in enumerate(
        zip([u_hbm] + table_hbms, (u_ref, fh_ref, fl_ref, ih_ref, il_ref))
    ):
        late.append(pltpu.make_async_copy(source, target, sems.at[bands + index]))
    for fetch in fetches + late:
        fetch.start()
    for fetch in fetches:
        fetch.wait()

    def forward(index, carry):
        start = pl.multiple_of(index * 16, 16)
        rows = pl.ds(start, 16)
        below = pl.ds(pl.multiple_of(start + MINOR, 16), 16)
        for tile in range(tiles):
            patch = special and tile == 0

            def load(a, tile=tile, patch=patch):
                pos_re, pos_im, neg_re, neg_im = [
                    x_ref[a, rows, MINOR * i : MINOR * (i + 1)].astype(F32) for i in range(4 * tile, 4 * tile + 4)
                ]
                if patch:
                    neg_re = jnp.where(own, pos_re, neg_re)
                    neg_im = jnp.where(own, pos_im, neg_im)
                return (pos_re + neg_re, pos_im - neg_im), (pos_im + neg_im, neg_re - pos_re)

            for b in range(8):
                values = [load(8 * a + b) for a in range(2)]
                for frame in range(2):
                    part = dft4_half([value[frame] for value in values])
                    dft32_first(part, b, mid_ref.at[2 * tile + frame])
            for frame in range(2):

                def store(k, re, im, tile=tile, frame=frame):
                    lanes = slice(MINOR * (2 * tile + frame), MINOR * (2 * tile + frame + 1))
                    xs_ref[k, rows, lanes] = re.astype(BF16)
                    xs_ref[k, below, lanes] = im.astype(BF16)

                dft32_last(store, mid_ref.at[2 * tile + frame])
        return carry

    lax.fori_loop(0, MINOR // 16, forward, 0)
    for fetch in late:
        fetch.wait()

    along_v = [[v_ref[tile, i : i + 1, :] for i in range(4)] for tile in range(tiles)]

    def middle(k):
        values = xs_ref[k]
        table = jnp.concatenate([fh_ref[k], fl_ref[k]], axis=1)
        spectra = dot(table, jnp.concatenate([values, values], axis=0))
        column = u_ref[k]
        along_u = [column[:, i : i + 1] for i in range(4)]
        parts_re, parts_im = [], []
        for tile in range(tiles):
            sin_even = along_u[0] * along_v[tile][1] + along_u[1] * along_v[tile][0]
            sin_odd = along_u[2] * along_v[tile][3] + along_u[3] * along_v[tile][2]
            scale = 1.0 / (4.0 * (sin_even * sin_even + sin_odd * sin_odd) + 2.0 * alpha_reg)
            sin_even = sin_even * scale
            sin_odd = sin_odd * scale
            even = slice(2 * MINOR * tile, 2 * MINOR * tile + MINOR)
            odd = slice(2 * MINOR * tile + MINOR, 2 * MINOR * (tile + 1))
            phase_re = sin_even * spectra[:MINOR, even] + sin_odd * spectra[:MINOR, odd]
            phase_im = sin_even * spectra[MINOR:, even] + sin_odd * spectra[MINOR:, odd]
            parts_re.append(phase_re.astype(BF16))
            parts_im.append(phase_im.astype(BF16))
        phase = jnp.concatenate([jnp.concatenate(parts_re, axis=1), jnp.concatenate(parts_im, axis=1)], axis=0)
        table = jnp.concatenate([ih_ref[k], il_ref[k]], axis=1)
        ys_ref[k] = dot(table, jnp.concatenate([phase, phase], axis=0))

    def middles(index, carry):
        for step in range(2):
            middle(2 * index + step)
        return carry

    lax.fori_loop(0, MAJOR // 2, middles, 0)

    def inverse(index, carry):
        start = pl.multiple_of(index * 16, 16)
        rows = pl.ds(start, 16)
        below = pl.ds(pl.multiple_of(start + MINOR, 16), 16)
        for tile in range(tiles):
            lanes = slice(MINOR * tile, MINOR * (tile + 1))
            patch = special and tile == 0

            def load(k, lanes=lanes):
                return ys_ref[k, below, lanes], ys_ref[k, rows, lanes]

            def store(a, im, re, tile=tile, patch=patch):
                if patch:
                    im = jnp.where(own, nyquist_ref[rows, a : a + 1], im)
                first = slice(2 * MINOR * tile, 2 * MINOR * tile + MINOR)
                second = slice(2 * MINOR * tile + MINOR, 2 * MINOR * (tile + 1))
                if a < HALF:
                    near_ref[a, rows, first] = re
                    near_ref[a, rows, second] = im
                else:
                    far_ref[a - HALF, rows, first] = re.astype(BF16)
                    far_ref[a - HALF, rows, second] = im.astype(BF16)

            dft32(load, store, mid_ref.at[tile])
        return carry

    lax.fori_loop(0, MINOR // 16, inverse, 0)


def columns(blocks, band, along_u, along_v, nyquist, after):
    tiles = along_v.shape[0]
    (fh, fl), (ih, il) = column_tables()
    special = nyquist is not None
    bands = len(blocks)
    operands = [band, along_v, *blocks, along_u] + [jnp.asarray(t) for t in (fh, fl, ih, il)] + after
    in_specs = [pl.BlockSpec(memory_space=pltpu.SMEM), whole_spec()] + [any_spec()] * (bands + 5 + len(after))
    if special:
        operands.append(nyquist)
        in_specs.append(whole_spec())
    shape = (HALF, MINOR, tiles * 2 * MINOR)
    return pl.pallas_call(
        functools.partial(column_kernel, special, tiles, bands, len(after)),
        in_specs=in_specs,
        out_specs=[whole_spec()] * 2,
        out_shape=[jax.ShapeDtypeStruct(shape, F32), jax.ShapeDtypeStruct(shape, BF16)],
        scratch_shapes=[
            pltpu.VMEM((2 * tiles, 64, 16, MINOR), F32),
            pltpu.VMEM((MAJOR, 2 * MINOR, tiles * 2 * MINOR), BF16),
            pltpu.VMEM((MAJOR, 2 * MINOR, tiles * MINOR), F32),
            pltpu.VMEM((HALF, MINOR, tiles * 4 * MINOR), BF16),
            pltpu.VMEM(along_u.shape, F32),
        ]
        + [pltpu.VMEM(fh.shape, BF16)] * 4
        + [pltpu.SemaphoreType.DMA((bands + 5,))],
        compiler_params=pltpu.CompilerParams(vmem_limit_bytes=58 * MIB),
        cost_estimate=pl.CostEstimate(
            flops=tiles * 64 * 32 * 8 * 256 * 256 * 256, bytes_accessed=30 * MIB, transcendentals=0
        ),
        name="columns",
    )(*operands)


def share_kernel(near_ref, far_ref, *rest):
    rest[-1][...] = (near_ref[...] + far_ref[...].astype(F32)).astype(BF16)


def add_shares(near, far, after):
    block = (4,) + near.shape[1:]
    spec = pl.BlockSpec(block, lambda i: (i, 0, 0))
    return pl.pallas_call(
        share_kernel,
        grid=(near.shape[0] // 4,),
        in_specs=[spec, spec] + [any_spec()] * len(after),
        out_specs=spec,
        out_shape=jax.ShapeDtypeStruct(near.shape, BF16),
        compiler_params=pltpu.CompilerParams(vmem_limit_bytes=58 * MIB),
        name="add_shares",
    )(near, far, *after)


def final_kernel(plan, bands, place_ref, *rest):
    ins, (high_ref, low_ref, out_ref, xs_ref, zs_ref) = rest[: len(plan)], rest[len(plan) :]
    place = place_ref[...]
    count = place.shape[0]
    width = 2 * MINOR
    for chunk, slots in enumerate(plan):
        for tile, slot in enumerate(slots):
            for band in range(bands):
                values = ins[chunk][band, :, :, width * tile : width * (tile + 1)].reshape(count, width)
                xs_ref[slot * bands + band] = dot(place, values).astype(BF16)

    for t in range(HALF):
        partner = (HALF - t) % HALF
        pair = jnp.concatenate([xs_ref[t], xs_ref[partner]], axis=1)
        pair = jnp.concatenate([pair, pair], axis=1)
        zs_ref[t] = dot(pair, jnp.concatenate([high_ref[t], low_ref[t]], axis=0))

    def group(index, carry):
        for half in range(2):
            rows = pl.ds(pl.multiple_of(index * 16 + 8 * half, 8), 8)
            values = [(zs_ref[t, rows, MINOR:], zs_ref[t, rows, :MINOR]) for t in range(HALF)]
            for n, (odd, even) in enumerate(dft16(values)):
                out_ref[rows, MINOR * 2 * n : MINOR * (2 * n + 1)] = even
                out_ref[rows, MINOR * (2 * n + 1) : MINOR * (2 * n + 2)] = odd
        return carry

    lax.fori_loop(0, count // 16, group, 0)


def rows_inverse(received, proj_order, bands, plan):
    _, projections, rows, _ = received[0].shape
    block = min(256 // projections, rows)
    count = block * projections
    high, low = final_tables()
    to = jnp.arange(count, dtype=jnp.int32)
    slot = proj_order[to // block]
    place = (to[:, None] == ((to % block) * projections + slot)[None, :]).astype(BF16)
    result = pl.pallas_call(
        functools.partial(final_kernel, plan, bands),
        grid=(rows // block,),
        in_specs=[fixed_spec((count, count))]
        + [pl.BlockSpec((bands, projections, block, each.shape[3]), lambda i: (0, 0, i, 0)) for each in received]
        + [fixed_spec(high.shape), fixed_spec(low.shape)],
        out_specs=pl.BlockSpec((count, LENGTH), lambda i: (i, 0)),
        out_shape=jax.ShapeDtypeStruct((rows * projections, LENGTH), F32),
        scratch_shapes=[
            pltpu.VMEM((HALF, count, 2 * MINOR), BF16),
            pltpu.VMEM((HALF, count, 2 * MINOR), F32),
        ],
        compiler_params=pltpu.CompilerParams(vmem_limit_bytes=56 * MIB),
        cost_estimate=pl.CostEstimate(
            flops=rows * projections * 16 * 10 * 256 * 256,
            bytes_accessed=rows * projections * LENGTH * 6 + 8 * MIB,
            transcendentals=0,
        ),
        name="rows_inverse",
    )(place, *received, jnp.asarray(high), jnp.asarray(low))
    return result.reshape(rows, projections, LENGTH)


def folded_square(position, length):
    folded = jnp.minimum(position, length - position).astype(F32) / length
    return folded * folded


def nyquist_column(re, im, coefficient):
    side = 64
    index = np.arange(side)
    angle = 2 * math.pi * np.outer(index, index) / side
    cosine, sine = np.cos(angle), np.sin(angle)
    forward = np.stack([np.stack([cosine, -sine], 1), np.stack([sine, cosine], 1)]).astype(np.float32)
    inverse = np.stack([np.stack([cosine, sine], 1), np.stack([-sine, cosine], 1)]).astype(np.float32)
    twist = 2 * math.pi * np.outer(index, index) / LENGTH
    twist_cos, twist_sin = np.cos(twist).astype(np.float32), np.sin(twist).astype(np.float32)
    contract = functools.partial(jnp.einsum, precision=lax.Precision.HIGHEST, preferred_element_type=F32)
    values = jnp.stack([re, im]).reshape(2, side, side)
    values = contract("cab,cadk->dkb", values, forward)
    values = jnp.stack(
        [values[0] * twist_cos + values[1] * twist_sin, values[1] * twist_cos - values[0] * twist_sin]
    )
    values = contract("ckb,cbdm->dkm", values, forward)
    position = (
        lax.broadcasted_iota(jnp.int32, (side, side), 0) + side * lax.broadcasted_iota(jnp.int32, (side, side), 1)
    )
    freq_sq = folded_square(position, LENGTH) + 0.25
    sines = jnp.sin(math.pi * coefficient[:, None, None] * freq_sq)
    scale = 1.0 / (2.0 * (sines[0] * sines[0] + sines[1] * sines[1]) + alpha_reg)
    values = jnp.stack(
        [
            (sines[0] * values[0] + sines[1] * values[1]) * scale,
            (sines[0] * values[1] - sines[1] * values[0]) * scale,
        ]
    )
    values = contract("ckm,cmdb->dkb", values, inverse)
    values = jnp.stack(
        [values[0] * twist_cos - values[1] * twist_sin, values[1] * twist_cos + values[0] * twist_sin]
    )
    column = contract("ckb,cka->ab", values, inverse[:, :, 0, :])
    return column.reshape(MAJOR, MINOR).T


def on_device(intensities, dist_index, fresnel_table, proj_order):
    rows = intensities.shape[2]
    halves = lax.axis_size("half")
    bands = lax.axis_size("inner")
    projections = lax.axis_size("proj")
    band = lax.axis_index("inner")
    slots = HALF // bands
    plan = chunk_plan(slots)
    totals = lax.psum(frame_sums(intensities), ("half", "inner"))
    scale = (rows * bands * halves * LENGTH) / totals

    here = jnp.asarray(band, jnp.int32).reshape(1)
    spectra = rows_forward(intensities, scale, here, bands, plan)

    table_size = fresnel_table.shape[0]
    onehot = (dist_index[0][:, None] == jnp.arange(table_size, dtype=jnp.int32)[None, :]).astype(F32)
    coefficient = jnp.sum(onehot * fresnel_table[None, :], axis=1)
    k_index = lax.broadcasted_iota(jnp.int32, (MAJOR, MINOR), 0)
    s_index = lax.broadcasted_iota(jnp.int32, (MAJOR, MINOR), 1)
    angle_u = math.pi * coefficient[:, None, None] * folded_square(k_index + MAJOR * s_index, LENGTH)
    along_u = jnp.stack([jnp.sin(angle_u[0]), jnp.cos(angle_u[0]), jnp.sin(angle_u[1]), jnp.cos(angle_u[1])], axis=-1)
    tile = jnp.asarray(sum(plan, []), jnp.int32)[:, None] * bands + band
    lane = jnp.arange(MINOR, dtype=jnp.int32)[None, :]
    first_tile = jnp.where(lane < MINOR // 2, MAJOR * lane, HALF + MAJOR * (lane - MINOR // 2))
    position_v = jnp.where(tile == 0, first_tile, tile + MAJOR * lane)
    angle_v = math.pi * coefficient[:, None, None] * folded_square(position_v, LENGTH)
    along_v = jnp.stack([jnp.sin(angle_v[0]), jnp.cos(angle_v[0]), jnp.sin(angle_v[1]), jnp.cos(angle_v[1])], axis=1)

    rows_to = LENGTH // (halves * bands * projections)
    received, pending, after = [], [], []

    def deliver(near, from_other, earlier):
        phase = add_shares(near, from_other, earlier)
        send = phase.reshape(bands * projections, rows_to, phase.shape[2])
        back = lax.all_to_all(send, ("inner", "proj"), split_axis=0, concat_axis=0, tiled=True)
        received.append(back.reshape(bands, projections, rows_to, phase.shape[2]))
        return phase

    for chunk, members in enumerate(plan):
        blocks = []
        for offset in range(bands):
            block = spectra[chunk * bands + offset]
            if offset:
                block = lax.ppermute(block, "inner", [(source, source ^ offset) for source in range(bands)])
            blocks.append(block)
        nyquist = None
        if chunk == special_chunk(plan):
            sent = jnp.stack([block[:, 2 * MINOR : 4 * MINOR : MINOR] for block in blocks]).astype(F32)
            sent = sent[jnp.arange(bands, dtype=jnp.int32) ^ band].reshape(bands * rows, 2)
            sent = jnp.pad(sent, ((0, bands * rows), (0, 0)))
            nyquist = nyquist_column(sent[:, 0], sent[:, 1], coefficient)
        width = len(members) * 4 * MINOR
        start = sum(len(each) for each in plan[:chunk])
        blocks = [block.reshape(-1, MINOR, width) for block in blocks]
        near, far = columns(blocks, here, along_u, along_v[start : start + len(members)], nyquist, after)
        after = [far]
        if pending:
            after = received[-1:] + [deliver(*pending.pop(), [far])]
        pending.append((near, lax.ppermute(far, "half", [(0, 1), (1, 0)])))
    deliver(*pending.pop(), received[-1:])

    return rows_inverse(received, proj_order, bands, plan)


def solution(mesh):
    proj, band = mesh.devices.shape
    split = jax.sharding.Mesh(mesh.devices.reshape(proj, 2, band // 2), ("proj", "half", "inner"))
    in_specs = (P("proj", None, ("half", "inner"), None), P("proj", None), P(), P())
    out_specs = P(("half", "inner", "proj"), None, None)
    return jax.shard_map(
        on_device, mesh=split, in_specs=in_specs, out_specs=out_specs, check_vma=False
    )
```

```python
import functools
import math

import jax
import jax.numpy as jnp
import numpy as np
from jax import lax
from jax.experimental import pallas as pl
from jax.experimental.pallas import tpu as pltpu
from jax.sharding import PartitionSpec as P

alpha_reg = 0.1
LENGTH = 4096
MAJOR = 32
MINOR = 128
HALF = MAJOR // 2
F32 = jnp.float32
BF16 = jnp.bfloat16
MIB = 1 << 20


def split_table(table):
    high = table.astype(np.float32).astype(jnp.bfloat16)
    low = (table - high.astype(np.float64)).astype(np.float32).astype(jnp.bfloat16)
    return high, low


def as_real(table):
    return np.block([[table.real, table.imag], [-table.imag, table.real]])


@functools.lru_cache(maxsize=None)
def step_tables():
    k = np.arange(MAJOR)[:, None, None]
    b = np.arange(MINOR)[None, :, None]
    s = np.arange(MINOR)[None, None, :]
    return np.exp(-2j * math.pi * ((b * (k + MAJOR * s)) % LENGTH) / LENGTH)


@functools.lru_cache(maxsize=None)
def row_tables():
    step = step_tables()
    out = np.zeros((34, 2 * MINOR, 2 * MINOR))
    for t in range(1, HALF):
        out[2 * t] = as_real(step[t])
        out[2 * t + 1] = as_real(step[MAJOR - t][:, ::-1])
    half = MINOR // 2
    zero = np.zeros((MINOR, half), np.complex128)
    negative = step[0][:, (-np.arange(half)) % MINOR].copy()
    negative[:, 0] = step[0][:, half]
    out[0] = as_real(np.concatenate([step[0][:, :half], zero], 1))
    out[1] = as_real(np.concatenate([negative, zero], 1))
    out[32] = as_real(np.concatenate([zero, step[HALF][:, :half]], 1))
    out[33] = as_real(np.concatenate([zero, step[HALF][:, ::-1][:, :half]], 1))
    return split_table(out)


@functools.lru_cache(maxsize=None)
def column_tables():
    inverse = np.stack([as_real(table) for table in step_tables()])
    return split_table(inverse.transpose(0, 2, 1)), split_table(inverse)


@functools.lru_cache(maxsize=None)
def final_tables():
    step = step_tables()
    out = np.zeros((HALF, 4 * MINOR, 2 * MINOR))
    eye = np.eye(MINOR)
    conjugate = np.diag(np.concatenate([np.ones(MINOR), -np.ones(MINOR)]))
    for t in range(1, HALF):
        turn = np.exp(2j * math.pi * t / MAJOR)
        out[t, : 2 * MINOR] = as_real((1 + 1j * turn) * np.conj(step[t]).T)
        partner = as_real(np.conj(step[HALF - t]).T)
        out[t, 2 * MINOR :] = partner @ conjugate @ as_real((1 - 1j * turn) * eye)
    half = MINOR // 2
    b = np.arange(MINOR)[None, :]
    s = np.arange(half)[:, None]
    even = 2 * math.pi * (b * s) / MINOR
    odd = 2 * math.pi * (b * (HALF + MAJOR * s)) / LENGTH
    first_re, first_im = 2 * np.cos(even), -2 * np.sin(even)
    first_re[0] = 1.0
    first_im[0] = (-1.0) ** np.arange(MINOR)
    second_re, second_im = 2 * np.cos(odd), -2 * np.sin(odd)
    first = np.concatenate([first_re, 0 * second_re, first_im, 0 * second_im], 0)
    second = np.concatenate([0 * first_re, second_re, 0 * first_im, second_im], 0)
    out[0, : 2 * MINOR] = np.concatenate([first + second, first - second], 1)
    return split_table(out / float(LENGTH * LENGTH))


def add(x, y):
    return (x[0] + y[0], x[1] + y[1])


def sub(x, y):
    return (x[0] - y[0], x[1] - y[1])


def turn(x, index, length):
    index = index % length
    re, im = x
    if index == 0:
        return x
    if 4 * index == length:
        return (im, -re)
    if 2 * index == length:
        return (-re, -im)
    if 4 * index == 3 * length:
        return (-im, re)
    angle = 2.0 * math.pi * index / length
    cosine, sine = math.cos(angle), math.sin(angle)
    if 8 * index == length:
        return ((re + im) * cosine, (im - re) * cosine)
    if 8 * index == 3 * length:
        return ((im - re) * sine, (re + im) * (-sine))
    return (re * cosine + im * sine, im * cosine - re * sine)


def dft4(x):
    a, b = add(x[0], x[2]), sub(x[0], x[2])
    c, d = add(x[1], x[3]), sub(x[1], x[3])
    return [add(a, c), (b[0] + d[1], b[1] - d[0]), sub(a, c), (b[0] - d[1], b[1] + d[0])]


def dft8(x):
    even, odd = dft4(x[0::2]), dft4(x[1::2])
    odd = [turn(value, index, 8) for index, value in enumerate(odd)]
    return [add(e, o) for e, o in zip(even, odd)] + [sub(e, o) for e, o in zip(even, odd)]


def dft16(x):
    middle = [dft4([x[4 * a + b] for a in range(4)]) for b in range(4)]
    out = [None] * 16
    for k in range(4):
        part = dft4([turn(middle[b][k], b * k, 16) for b in range(4)])
        for m in range(4):
            out[k + 4 * m] = part[m]
    return out


def dft4_half(x):
    return [add(x[0], x[1]), (x[0][0] + x[1][1], x[0][1] - x[1][0]), sub(x[0], x[1]), (x[0][0] - x[1][1], x[0][1] + x[1][0])]


def dft32_first(part, b, mid_ref):
    for k in range(4):
        re, im = turn(part[k], b * k, 32)
        mid_ref[2 * (8 * k + b)] = re
        mid_ref[2 * (8 * k + b) + 1] = im


def dft32_last(store, mid_ref):
    for k in range(4):
        part = dft8([(mid_ref[2 * (8 * k + b)], mid_ref[2 * (8 * k + b) + 1]) for b in range(8)])
        for m in range(8):
            store(k + 4 * m, *part[m])


def dft32(load, store, mid_ref):
    for b in range(8):
        dft32_first(dft4([load(8 * a + b) for a in range(4)]), b, mid_ref)
    dft32_last(store, mid_ref)


def dot(x, y):
    return jnp.dot(x, y, preferred_element_type=F32)


def sum_kernel(x_ref, out_ref, total_ref):
    @pl.when(pl.program_id(0) == 0)
    def _():
        total_ref[...] = jnp.zeros_like(total_ref)

    rows = x_ref.shape[2]
    for frame in range(2):
        for start in range(0, LENGTH, 8 * MINOR):
            lanes = slice(start, start + 8 * MINOR)
            total = total_ref[frame, :, lanes]
            for row in range(0, rows, 16):
                values = x_ref[0, frame, row : row + 16, lanes].astype(F32)
                total = total + (values[:8] + values[8:])
            total_ref[frame, :, lanes] = total

    @pl.when(pl.program_id(0) == pl.num_programs(0) - 1)
    def _():
        for frame in range(2):
            out_ref[0, frame] = jnp.sum(total_ref[frame])


def frame_sums(intensities):
    rows = intensities.shape[2]
    block = 128
    return pl.pallas_call(
        sum_kernel,
        grid=(rows // block,),
        in_specs=[pl.BlockSpec((1, 2, block, LENGTH), lambda i: (0, 0, i, 0))],
        out_specs=pl.BlockSpec(memory_space=pltpu.SMEM),
        out_shape=jax.ShapeDtypeStruct((1, 2), F32),
        scratch_shapes=[pltpu.VMEM((2, 8, LENGTH), F32)],
        compiler_params=pltpu.CompilerParams(vmem_limit_bytes=58 * MIB),
        name="frame_sums",
    )(intensities)


def row_kernel(plan, bands, band_ref, scale_ref, x_ref, high_hbm, low_hbm, *rest):
    outs = rest[: len(plan) * bands]
    mid_ref, xs_ref, high_ref, low_ref, sems = rest[len(plan) * bands :]
    rows_here = x_ref.shape[2]
    band = band_ref[0]
    scale_even, scale_odd = scale_ref[0, 0], scale_ref[0, 1]

    def fetches():
        return [
            pltpu.make_async_copy(high_hbm, high_ref, sems.at[0]),
            pltpu.make_async_copy(low_hbm, low_ref, sems.at[1]),
        ]

    @pl.when(pl.program_id(0) == 0)
    def _():
        for fetch in fetches():
            fetch.start()

    def group(index, carry):
        rows = pl.ds(pl.multiple_of(index * 16, 16), 16)

        def load(a):
            lanes = slice(MINOR * a, MINOR * (a + 1))
            even = x_ref[0, 0, rows, lanes].astype(F32) * scale_even - 1.0
            odd = x_ref[0, 1, rows, lanes].astype(F32) * scale_odd - 1.0
            return even, odd

        def store(k, re, im):
            for place, value in enumerate((re, im)):
                high = value.astype(BF16)
                low = (value - high.astype(F32)).astype(BF16)
                xs_ref[k, rows, MINOR * place : MINOR * (place + 1)] = high
                xs_ref[k, rows, MINOR * (2 + place) : MINOR * (3 + place)] = low

        dft32(load, store, mid_ref)
        return carry

    lax.fori_loop(0, rows_here // 16, group, 0)

    @pl.when(pl.program_id(0) == 0)
    def _():
        for fetch in fetches():
            fetch.wait()

    def apply(k, table):
        values = xs_ref[k]
        high = high_ref[table]
        whole = jnp.concatenate([values, values[:, : 2 * MINOR]], axis=1)
        return dot(whole, jnp.concatenate([high, high, low_ref[table]], axis=0))

    width = 2 * MINOR
    for chunk, slots in enumerate(plan):
        for place, slot in enumerate(slots):
            start = 2 * width * place
            for offset in range(bands):
                t = slot * bands + (band ^ offset)
                out_ref = outs[chunk * bands + offset]
                out_ref[:, start : start + width] = apply(t, 2 * t).astype(BF16)
                out_ref[:, start + width : start + 2 * width] = apply(
                    lax.rem(MAJOR - t, MAJOR), 2 * t + 1
                ).astype(BF16)
    chunk = special_chunk(plan)
    for offset in range(bands):

        @pl.when(band == offset)
        def _(out_ref=outs[chunk * bands + offset]):
            out_ref[:, :width] = (apply(0, 0) + apply(HALF, 32)).astype(BF16)
            out_ref[:, width : 2 * width] = (apply(0, 1) + apply(HALF, 33)).astype(BF16)


def chunk_plan(count):
    if count < 8:
        return [[slot] for slot in range(1, count)] + [[0]]
    order = [1, 2, 3, 4, 0] + list(range(5, count))
    return [order[i : i + 2] for i in range(0, count, 2)]


def special_chunk(plan):
    return next(chunk for chunk, slots in enumerate(plan) if slots[0] == 0)


def whole_spec():
    return pl.BlockSpec(memory_space=pltpu.VMEM)


def any_spec():
    return pl.BlockSpec(memory_space=pl.ANY)


def fixed_spec(shape):
    return pl.BlockSpec(shape, lambda *_: (0,) * len(shape), pipeline_mode=pl.Buffered(1))


def rows_forward(intensities, scale, band, bands, plan):
    rows = intensities.shape[2]
    block = min(256, rows)
    high, low = row_tables()
    widths = [len(slots) * 4 * MINOR for slots in plan for _ in range(bands)]
    return pl.pallas_call(
        functools.partial(row_kernel, plan, bands),
        grid=(rows // block,),
        in_specs=[
            pl.BlockSpec(memory_space=pltpu.SMEM),
            pl.BlockSpec(memory_space=pltpu.SMEM),
            pl.BlockSpec((1, 2, block, LENGTH), lambda i: (0, 0, i, 0)),
            any_spec(),
            any_spec(),
        ],
        out_specs=[pl.BlockSpec((block, width), lambda i: (i, 0)) for width in widths],
        out_shape=[jax.ShapeDtypeStruct((rows, width), BF16) for width in widths],
        scratch_shapes=[
            pltpu.VMEM((64, 16, MINOR), F32),
            pltpu.VMEM((MAJOR, block, 4 * MINOR), BF16),
            pltpu.VMEM(high.shape, BF16),
            pltpu.VMEM(low.shape, BF16),
            pltpu.SemaphoreType.DMA((2,)),
        ],
        compiler_params=pltpu.CompilerParams(vmem_limit_bytes=58 * MIB),
        cost_estimate=pl.CostEstimate(
            flops=64 * rows * 34 * 6 * 256 * 256, bytes_accessed=4 * rows * LENGTH * 2 + 9 * MIB, transcendentals=0
        ),
        name="rows_forward",
    )(band, scale, intensities, jnp.asarray(high), jnp.asarray(low))


def column_kernel(special, tiles, bands, waits, band_ref, v_ref, *rest):
    blocks = rest[:bands]
    u_hbm, *table_hbms = rest[bands : bands + 5]
    rest = rest[bands + 5 + waits :]
    band = band_ref[0]
    if special:
        nyquist_ref, *rest = rest
        lane = lax.broadcasted_iota(jnp.int32, (16, MINOR), 1)
        own = (lane == 0) & (band == 0)
    near_ref, far_ref, mid_ref, xs_ref, ys_ref, x_ref, u_ref, fh_ref, fl_ref, ih_ref, il_ref, sems = rest

    fetches = []
    height = HALF // bands
    for offset in range(bands):
        start = (band ^ offset) * height
        fetches.append(pltpu.make_async_copy(blocks[offset], x_ref.at[pl.ds(start, height)], sems.at[offset]))
    late = []
    for index, (source, target) in enumerate(
        zip([u_hbm] + table_hbms, (u_ref, fh_ref, fl_ref, ih_ref, il_ref))
    ):
        late.append(pltpu.make_async_copy(source, target, sems.at[bands + index]))
    for fetch in fetches + late:
        fetch.start()
    for fetch in fetches:
        fetch.wait()

    def forward(index, carry):
        start = pl.multiple_of(index * 16, 16)
        rows = pl.ds(start, 16)
        below = pl.ds(pl.multiple_of(start + MINOR, 16), 16)
        for tile in range(tiles):
            patch = special and tile == 0

            def load(a, tile=tile, patch=patch):
                pos_re, pos_im, neg_re, neg_im = [
                    x_ref[a, rows, MINOR * i : MINOR * (i + 1)].astype(F32) for i in range(4 * tile, 4 * tile + 4)
                ]
                if patch:
                    neg_re = jnp.where(own, pos_re, neg_re)
                    neg_im = jnp.where(own, pos_im, neg_im)
                return (pos_re + neg_re, pos_im - neg_im), (pos_im + neg_im, neg_re - pos_re)

            for b in range(8):
                values = [load(8 * a + b) for a in range(2)]
                for frame in range(2):
                    part = dft4_half([value[frame] for value in values])
                    dft32_first(part, b, mid_ref.at[2 * tile + frame])
            for frame in range(2):

                def store(k, re, im, tile=tile, frame=frame):
                    lanes = slice(MINOR * (2 * tile + frame), MINOR * (2 * tile + frame + 1))
                    xs_ref[k, rows, lanes] = re.astype(BF16)
                    xs_ref[k, below, lanes] = im.astype(BF16)

                dft32_last(store, mid_ref.at[2 * tile + frame])
        return carry

    lax.fori_loop(0, MINOR // 16, forward, 0)
    for fetch in late:
        fetch.wait()

    along_v = [[v_ref[tile, i : i + 1, :] for i in range(4)] for tile in range(tiles)]

    def middle(k):
        values = xs_ref[k]
        table = jnp.concatenate([fh_ref[k], fl_ref[k]], axis=1)
        spectra = dot(table, jnp.concatenate([values, values], axis=0))
        column = u_ref[k]
        along_u = [column[:, i : i + 1] for i in range(4)]
        parts_re, parts_im = [], []
        for tile in range(tiles):
            sin_even = along_u[0] * along_v[tile][1] + along_u[1] * along_v[tile][0]
            sin_odd = along_u[2] * along_v[tile][3] + along_u[3] * along_v[tile][2]
            scale = 1.0 / (4.0 * (sin_even * sin_even + sin_odd * sin_odd) + 2.0 * alpha_reg)
            sin_even = sin_even * scale
            sin_odd = sin_odd * scale
            even = slice(2 * MINOR * tile, 2 * MINOR * tile + MINOR)
            odd = slice(2 * MINOR * tile + MINOR, 2 * MINOR * (tile + 1))
            phase_re = sin_even * spectra[:MINOR, even] + sin_odd * spectra[:MINOR, odd]
            phase_im = sin_even * spectra[MINOR:, even] + sin_odd * spectra[MINOR:, odd]
            parts_re.append(phase_re.astype(BF16))
            parts_im.append(phase_im.astype(BF16))
        phase = jnp.concatenate([jnp.concatenate(parts_re, axis=1), jnp.concatenate(parts_im, axis=1)], axis=0)
        table = jnp.concatenate([ih_ref[k], il_ref[k]], axis=1)
        ys_ref[k] = dot(table, jnp.concatenate([phase, phase], axis=0))

    def middles(index, carry):
        for step in range(2):
            middle(2 * index + step)
        return carry

    lax.fori_loop(0, MAJOR // 2, middles, 0)

    def inverse(index, carry):
        start = pl.multiple_of(index * 16, 16)
        rows = pl.ds(start, 16)
        below = pl.ds(pl.multiple_of(start + MINOR, 16), 16)
        for tile in range(tiles):
            lanes = slice(MINOR * tile, MINOR * (tile + 1))
            patch = special and tile == 0

            def load(k, lanes=lanes):
                return ys_ref[k, below, lanes], ys_ref[k, rows, lanes]

            def store(a, im, re, tile=tile, patch=patch):
                if patch:
                    im = jnp.where(own, nyquist_ref[rows, a : a + 1], im)
                first = slice(2 * MINOR * tile, 2 * MINOR * tile + MINOR)
                second = slice(2 * MINOR * tile + MINOR, 2 * MINOR * (tile + 1))
                if a < HALF:
                    near_ref[a, rows, first] = re
                    near_ref[a, rows, second] = im
                else:
                    far_ref[a - HALF, rows, first] = re.astype(BF16)
                    far_ref[a - HALF, rows, second] = im.astype(BF16)

            dft32(load, store, mid_ref.at[tile])
        return carry

    lax.fori_loop(0, MINOR // 16, inverse, 0)


def columns(blocks, band, along_u, along_v, nyquist, after):
    tiles = along_v.shape[0]
    (fh, fl), (ih, il) = column_tables()
    special = nyquist is not None
    bands = len(blocks)
    operands = [band, along_v, *blocks, along_u] + [jnp.asarray(t) for t in (fh, fl, ih, il)] + after
    in_specs = [pl.BlockSpec(memory_space=pltpu.SMEM), whole_spec()] + [any_spec()] * (bands + 5 + len(after))
    if special:
        operands.append(nyquist)
        in_specs.append(whole_spec())
    shape = (HALF, MINOR, tiles * 2 * MINOR)
    return pl.pallas_call(
        functools.partial(column_kernel, special, tiles, bands, len(after)),
        in_specs=in_specs,
        out_specs=[whole_spec()] * 2,
        out_shape=[jax.ShapeDtypeStruct(shape, F32), jax.ShapeDtypeStruct(shape, BF16)],
        scratch_shapes=[
            pltpu.VMEM((2 * tiles, 64, 16, MINOR), F32),
            pltpu.VMEM((MAJOR, 2 * MINOR, tiles * 2 * MINOR), BF16),
            pltpu.VMEM((MAJOR, 2 * MINOR, tiles * MINOR), F32),
            pltpu.VMEM((HALF, MINOR, tiles * 4 * MINOR), BF16),
            pltpu.VMEM(along_u.shape, F32),
        ]
        + [pltpu.VMEM(fh.shape, BF16)] * 4
        + [pltpu.SemaphoreType.DMA((bands + 5,))],
        compiler_params=pltpu.CompilerParams(vmem_limit_bytes=58 * MIB),
        cost_estimate=pl.CostEstimate(
            flops=tiles * 64 * 32 * 8 * 256 * 256 * 256, bytes_accessed=30 * MIB, transcendentals=0
        ),
        name="columns",
    )(*operands)


def share_kernel(near_ref, far_ref, *rest):
    rest[-1][...] = (near_ref[...] + far_ref[...].astype(F32)).astype(BF16)


def add_shares(near, far, after):
    block = (4,) + near.shape[1:]
    spec = pl.BlockSpec(block, lambda i: (i, 0, 0))
    return pl.pallas_call(
        share_kernel,
        grid=(near.shape[0] // 4,),
        in_specs=[spec, spec] + [any_spec()] * len(after),
        out_specs=spec,
        out_shape=jax.ShapeDtypeStruct(near.shape, BF16),
        compiler_params=pltpu.CompilerParams(vmem_limit_bytes=58 * MIB),
        name="add_shares",
    )(near, far, *after)


def final_kernel(plan, bands, place_ref, *rest):
    ins, (high_ref, low_ref, out_ref, xs_ref, zs_ref) = rest[: len(plan)], rest[len(plan) :]
    place = place_ref[...]
    count = place.shape[0]
    width = 2 * MINOR
    for chunk, slots in enumerate(plan):
        for tile, slot in enumerate(slots):
            for band in range(bands):
                values = ins[chunk][band, :, :, width * tile : width * (tile + 1)].reshape(count, width)
                xs_ref[slot * bands + band] = dot(place, values).astype(BF16)

    for t in range(HALF):
        partner = (HALF - t) % HALF
        pair = jnp.concatenate([xs_ref[t], xs_ref[partner]], axis=1)
        pair = jnp.concatenate([pair, pair], axis=1)
        zs_ref[t] = dot(pair, jnp.concatenate([high_ref[t], low_ref[t]], axis=0))

    def group(index, carry):
        for half in range(2):
            rows = pl.ds(pl.multiple_of(index * 16 + 8 * half, 8), 8)
            values = [(zs_ref[t, rows, MINOR:], zs_ref[t, rows, :MINOR]) for t in range(HALF)]
            for n, (odd, even) in enumerate(dft16(values)):
                out_ref[rows, MINOR * 2 * n : MINOR * (2 * n + 1)] = even
                out_ref[rows, MINOR * (2 * n + 1) : MINOR * (2 * n + 2)] = odd
        return carry

    lax.fori_loop(0, count // 16, group, 0)


def rows_inverse(received, proj_order, bands, plan):
    _, projections, rows, _ = received[0].shape
    block = min(256 // projections, rows)
    count = block * projections
    high, low = final_tables()
    to = jnp.arange(count, dtype=jnp.int32)
    slot = proj_order[to // block]
    place = (to[:, None] == ((to % block) * projections + slot)[None, :]).astype(BF16)
    result = pl.pallas_call(
        functools.partial(final_kernel, plan, bands),
        grid=(rows // block,),
        in_specs=[fixed_spec((count, count))]
        + [pl.BlockSpec((bands, projections, block, each.shape[3]), lambda i: (0, 0, i, 0)) for each in received]
        + [fixed_spec(high.shape), fixed_spec(low.shape)],
        out_specs=pl.BlockSpec((count, LENGTH), lambda i: (i, 0)),
        out_shape=jax.ShapeDtypeStruct((rows * projections, LENGTH), F32),
        scratch_shapes=[
            pltpu.VMEM((HALF, count, 2 * MINOR), BF16),
            pltpu.VMEM((HALF, count, 2 * MINOR), F32),
        ],
        compiler_params=pltpu.CompilerParams(vmem_limit_bytes=56 * MIB),
        cost_estimate=pl.CostEstimate(
            flops=rows * projections * 16 * 10 * 256 * 256,
            bytes_accessed=rows * projections * LENGTH * 6 + 8 * MIB,
            transcendentals=0,
        ),
        name="rows_inverse",
    )(place, *received, jnp.asarray(high), jnp.asarray(low))
    return result.reshape(rows, projections, LENGTH)


def folded_square(position, length):
    folded = jnp.minimum(position, length - position).astype(F32) / length
    return folded * folded


def nyquist_column(re, im, coefficient):
    side = 64
    index = np.arange(side)
    angle = 2 * math.pi * np.outer(index, index) / side
    cosine, sine = np.cos(angle), np.sin(angle)
    forward = np.stack([np.stack([cosine, -sine], 1), np.stack([sine, cosine], 1)]).astype(np.float32)
    inverse = np.stack([np.stack([cosine, sine], 1), np.stack([-sine, cosine], 1)]).astype(np.float32)
    twist = 2 * math.pi * np.outer(index, index) / LENGTH
    twist_cos, twist_sin = np.cos(twist).astype(np.float32), np.sin(twist).astype(np.float32)
    contract = functools.partial(jnp.einsum, precision=lax.Precision.HIGHEST, preferred_element_type=F32)
    values = jnp.stack([re, im]).reshape(2, side, side)
    values = contract("cab,cadk->dkb", values, forward)
    values = jnp.stack(
        [values[0] * twist_cos + values[1] * twist_sin, values[1] * twist_cos - values[0] * twist_sin]
    )
    values = contract("ckb,cbdm->dkm", values, forward)
    position = (
        lax.broadcasted_iota(jnp.int32, (side, side), 0) + side * lax.broadcasted_iota(jnp.int32, (side, side), 1)
    )
    freq_sq = folded_square(position, LENGTH) + 0.25
    sines = jnp.sin(math.pi * coefficient[:, None, None] * freq_sq)
    scale = 1.0 / (2.0 * (sines[0] * sines[0] + sines[1] * sines[1]) + alpha_reg)
    values = jnp.stack(
        [
            (sines[0] * values[0] + sines[1] * values[1]) * scale,
            (sines[0] * values[1] - sines[1] * values[0]) * scale,
        ]
    )
    values = contract("ckm,cmdb->dkb", values, inverse)
    values = jnp.stack(
        [values[0] * twist_cos - values[1] * twist_sin, values[1] * twist_cos + values[0] * twist_sin]
    )
    column = contract("ckb,cka->ab", values, inverse[:, :, 0, :])
    return column.reshape(MAJOR, MINOR).T


def on_device(intensities, dist_index, fresnel_table, proj_order):
    rows = intensities.shape[2]
    halves = lax.axis_size("half")
    bands = lax.axis_size("inner")
    projections = lax.axis_size("proj")
    band = lax.axis_index("inner")
    slots = HALF // bands
    plan = chunk_plan(slots)
    totals = lax.psum(frame_sums(intensities), ("half", "inner"))
    scale = (rows * bands * halves * LENGTH) / totals

    here = jnp.asarray(band, jnp.int32).reshape(1)
    spectra = rows_forward(intensities, scale, here, bands, plan)

    table_size = fresnel_table.shape[0]
    onehot = (dist_index[0][:, None] == jnp.arange(table_size, dtype=jnp.int32)[None, :]).astype(F32)
    coefficient = jnp.sum(onehot * fresnel_table[None, :], axis=1)
    k_index = lax.broadcasted_iota(jnp.int32, (MAJOR, MINOR), 0)
    s_index = lax.broadcasted_iota(jnp.int32, (MAJOR, MINOR), 1)
    angle_u = math.pi * coefficient[:, None, None] * folded_square(k_index + MAJOR * s_index, LENGTH)
    along_u = jnp.stack([jnp.sin(angle_u[0]), jnp.cos(angle_u[0]), jnp.sin(angle_u[1]), jnp.cos(angle_u[1])], axis=-1)
    tile = jnp.asarray(sum(plan, []), jnp.int32)[:, None] * bands + band
    lane = jnp.arange(MINOR, dtype=jnp.int32)[None, :]
    first_tile = jnp.where(lane < MINOR // 2, MAJOR * lane, HALF + MAJOR * (lane - MINOR // 2))
    position_v = jnp.where(tile == 0, first_tile, tile + MAJOR * lane)
    angle_v = math.pi * coefficient[:, None, None] * folded_square(position_v, LENGTH)
    along_v = jnp.stack([jnp.sin(angle_v[0]), jnp.cos(angle_v[0]), jnp.sin(angle_v[1]), jnp.cos(angle_v[1])], axis=1)

    rows_to = LENGTH // (halves * bands * projections)
    received, pending, after = [], [], []

    def deliver(near, from_other, earlier):
        phase = add_shares(near, from_other, earlier)
        send = phase.reshape(bands * projections, rows_to, phase.shape[2])
        back = lax.all_to_all(send, ("inner", "proj"), split_axis=0, concat_axis=0, tiled=True)
        received.append(back.reshape(bands, projections, rows_to, phase.shape[2]))
        return phase

    for chunk, members in enumerate(plan):
        blocks = []
        for offset in range(bands):
            block = spectra[chunk * bands + offset]
            if offset:
                block = lax.ppermute(block, "inner", [(source, source ^ offset) for source in range(bands)])
            blocks.append(block)
        nyquist = None
        if chunk == special_chunk(plan):
            sent = jnp.stack([block[:, 2 * MINOR : 4 * MINOR : MINOR] for block in blocks]).astype(F32)
            sent = sent[jnp.arange(bands, dtype=jnp.int32) ^ band].reshape(bands * rows, 2)
            sent = jnp.pad(sent, ((0, bands * rows), (0, 0)))
            nyquist = nyquist_column(sent[:, 0], sent[:, 1], coefficient)
        width = len(members) * 4 * MINOR
        start = sum(len(each) for each in plan[:chunk])
        blocks = [block.reshape(-1, MINOR, width) for block in blocks]
        near, far = columns(blocks, here, along_u, along_v[start : start + len(members)], nyquist, after)
        after = [far]
        if pending:
            earlier = received[-1:]
            after = earlier + [deliver(*pending.pop(), [far] + (earlier if chunk > 2 else []))]
        pending.append((near, lax.ppermute(far, "half", [(0, 1), (1, 0)])))
    deliver(*pending.pop(), received[-1:])

    return rows_inverse(received, proj_order, bands, plan)


def solution(mesh):
    proj, band = mesh.devices.shape
    split = jax.sharding.Mesh(mesh.devices.reshape(proj, 2, band // 2), ("proj", "half", "inner"))
    in_specs = (P("proj", None, ("half", "inner"), None), P("proj", None), P(), P())
    out_specs = P(("half", "inner", "proj"), None, None)
    return jax.shard_map(
        on_device, mesh=split, in_specs=in_specs, out_specs=out_specs, check_vma=False
    )
```
